128 devices in a mesh: pipe: 4 (over x), tp: 8 (over y, z_hi), dp: 4 (over z_lo, core).
Axes of the slice: x: 4, y: 4, z: 4 (z_hi: 2, z_lo: 2; z = z_hi * 2 + z_lo), core: 2. Of those that a mesh axis runs over, the one named last changes fastest.
Arguments:
- upstream: bfloat16 [4, 6656, 8192], P('pipe', ('dp', 'tp')), may hold values from -6 to 6
- saved_input: bfloat16 [4, 2, 6656, 4096], P('pipe', None, 'dp', 'tp'), may hold values from -6 to 6
- weight: bfloat16 [4, 4096, 8192], P('pipe', 'tp', 'dp'), may hold values from -0.0625 to 0.0625
- weight_noise: bfloat16 [4, 4096, 8192], P('pipe', 'tp', 'dp'), may hold values from -0.03125 to 0.03125
- levels: int32 [4, 32, 64], P('pipe', 'tp', 'dp'), may hold values from 1 to 4
- plan: int32 [4], replicated, may hold values from 0 to 1
Outputs:
- master_grad: float32 [4, 4096, 8192], P('pipe', 'tp', 'dp')
- passed: bfloat16 [4, 6656, 4096], P('pipe', ('dp', 'tp'))
The draws below stay inside these ranges and needn't reach their ends.
All inputs are finite; a program needn't handle non-finite values.
Results may differ from the reference program's by a relative error of at most 0.015.
Values may be sent and summed in bfloat16 or wider, within the bound.
A program may use at most 192 MiB of HBM per device.

```python
import jax
import jax.numpy as jnp
from jax import lax

D = 8192
E = 4096
TILE = 128
MB = 2
TOK_DEV = 208
TOKENS = 6656
N_PIPE = 4
N_TP = 8
N_DP = 4


def place_ends(drawn, key, low, high):
    index_at = [jax.random.randint(jax.random.fold_in(key, axis), (), 0, length) for axis, length in enumerate(drawn.shape)]
    longest = drawn.shape.index(max(drawn.shape))
    next_to = index_at[:longest] + [(index_at[longest] + 1) % drawn.shape[longest]] + index_at[longest + 1:]
    return drawn.at[tuple(index_at)].set(low).at[tuple(next_to)].set(high)


def steps_of(own_key, shape, split, low, largest):
    def one(axis_at, shards_of):
        heights = jax.random.uniform(jax.random.fold_in(jax.random.fold_in(own_key, 6), axis_at), (shards_of,), jnp.float32, low / len(split), largest / len(split))
        return jnp.repeat(jnp.exp(heights), shape[axis_at] // shards_of).reshape((-1,) + (1,) * (len(shape) - axis_at - 1))

    factor_of = one(*split[0])
    for cut in split[1:]:
        factor_of = factor_of * one(*cut)
    return factor_of


def centred(own_key, extent, width, limit, split=(), held_as=jnp.bfloat16):
    drawn = jax.random.normal(own_key, extent, jnp.float32) * width
    if len(split) > 0:
        drawn = steps_of(own_key, extent, split, -0.22, 0.18) * drawn
    return jnp.clip(drawn, min=-limit, max=limit).astype(held_as)


def setup_inputs(seed: int = 0) -> dict:
    splits = jax.random.split(jax.random.key(seed), 7)
    return {
        "upstream": centred(splits[0], (N_PIPE, TOKENS, D), 1.0, 6.0, ((0, 4), (1, 32))),
        "saved_input": centred(splits[1], (N_PIPE, MB, TOKENS, E), 1.0, 6.0, ((0, 4), (2, 4), (3, 8))),
        "weight": centred(splits[2], (N_PIPE, E, D), D ** -0.5, 0.0625, ((0, 4), (1, 8), (2, 4))),
        "weight_noise": centred(splits[3], (N_PIPE, E, D), 0.006, 0.03125, ((0, 4), (1, 8), (2, 4))),
        "levels": place_ends(jax.random.randint(splits[4], (N_PIPE, E // TILE, D // TILE), 1, 5), jax.random.fold_in(splits[4], 1), 1, 4).astype(jnp.int32),
        "plan": place_ends(jax.random.randint(splits[5], (N_PIPE,), 0, MB), jax.random.fold_in(splits[5], 1), 0, MB - 1).astype(jnp.int32),
    }


clip_step = 0.006

def reference(upstream, saved_input, weight, weight_noise, levels, plan):
    masters = []
    outputs = []
    shard_rows = TOK_DEV * N_TP
    for section in range(N_PIPE):
        noisy = weight[section].astype(jnp.float32) + weight_noise[section].astype(jnp.float32)
        bounds = levels[section].astype(jnp.float32) * clip_step
        bounds = jnp.repeat(jnp.repeat(bounds, TILE, axis=0), TILE, axis=1)
        effective = jnp.clip(noisy, -bounds, bounds).astype(jnp.bfloat16)
        inside = (jnp.abs(noisy) <= bounds).astype(jnp.float32)
        chosen = saved_input[section][plan[section]]
        grad_in = upstream[section]
        branch = jnp.dot(grad_in, effective.T, preferred_element_type=jnp.float32).astype(jnp.bfloat16)
        summed = jnp.zeros((E, D), jnp.float32)
        for shard in range(N_DP):
            left = chosen[shard * shard_rows:(shard + 1) * shard_rows]
            right = grad_in[shard * shard_rows:(shard + 1) * shard_rows]
            partial_sum = lax.dot_general(left, right, (((0,), (0,)), ((), ())), preferred_element_type=jnp.float32)
            summed = summed + partial_sum.astype(jnp.bfloat16).astype(jnp.float32)
        masters.append(summed * inside / jnp.sqrt(jnp.float32(TOKENS)))
        outputs.append(branch)
    passed = outputs[1:] + [jnp.zeros_like(outputs[0])]
    return (jnp.stack(masters), jnp.stack(passed))
```

```python
import functools

import jax
import jax.numpy as jnp
from jax import lax
from jax.experimental import pallas as pl
from jax.experimental.pallas import tpu as pltpu
from jax.sharding import PartitionSpec as P

clip_step = 0.006
MESH = pl.DeviceIdType.MESH
TILE = 128


def aligned(start, size, step=128):
    return pl.ds(pl.multiple_of(start, step), size)


def relay_kernel(
    up, picked, weight, noise, levels,
    master, passed,
    ubuf, wbuf, cbuf, ctbuf, acc, gself, gopp, gside, ghalf, gfull, bsend, brecv, bout,
    u_loc, u_sib_s, u_sib_r, u_own_s, u_own_r, u_fwd_s, u_fwd_r,
    c_loc, c_opp_s, c_opp_r, c_sib_s, c_sib_r,
    w_own_s, w_own_r, w_fwd_s, w_fwd_r,
    g_half_s, g_half_r, g_full_s, g_full_r,
    b_sib_s, b_sib_r, b_out_s, b_out_r, m_out,
):
    tok = up.shape[0]
    rows = tok * 4
    quarter = weight.shape[1]
    blk = weight.shape[0]
    half = blk // 2
    subs = 4
    cw = quarter // subs
    feats = 2 * blk

    x = lax.axis_index("pipe")
    tp = lax.axis_index("tp")
    dp = lax.axis_index("dp")
    y, zh = tp // 2, tp % 2
    zl, c = dp // 2, dp % 2
    z = 2 * zh + zl
    oc = 1 - c

    def at(xx, yy, zz, cc):
        xx, yy, zz = xx % 4, yy % 4, zz % 4
        return (xx, yy * 2 + zz // 2, (zz % 2) * 2 + cc)

    sib = at(x, y, z, oc)
    opp = at(x, y, z + 2, c)
    ynb = (at(x, y + 1, z, c), at(x, y + 3, z, c))
    znb = (at(x, y, z + 1, c), at(x, y, z + 3, c))
    zp = (zh + zl) % 2
    zside = (zp, 1 - zp)

    barrier = pltpu.get_barrier_semaphore()
    greet = [sib, opp, *ynb, *znb] + [at(x + 1, y + j, z, c) for j in range(4)]
    for one in greet:
        pl.semaphore_signal(barrier, inc=1, device_id=one, device_id_type=MESH)

    def remote(src, dst, s, r, to):
        return pltpu.make_async_remote_copy(
            src_ref=src, dst_ref=dst, send_sem=s, recv_sem=r, device_id=to, device_id_type=MESH
        )

    def urow(yy, cc):
        return aligned(cc * rows + yy * tok, tok, 16)

    def ucol(k):
        return aligned((k % 2) * quarter + (k // 2) * cw, cw)

    def hcol(k, cc):
        return aligned(((zl + k) % 2) * (2 * quarter) + cc * quarter + (k // 2) * cw, cw)

    def u_local(k):
        return pltpu.make_async_copy(up.at[:, hcol(k, c)], ubuf.at[urow(y, c), ucol(k)], u_loc.at[k])

    def u_sib(k):
        return remote(up.at[:, hcol(k, oc)], ubuf.at[urow(y, c), ucol(k)], u_sib_s.at[k], u_sib_r.at[k], sib)

    def u_own(k, d, mine):
        cc = c if mine else oc
        src = up.at[:, hcol(k, c)] if mine else ubuf.at[urow(y, oc), ucol(k)]
        at_sem = (k, d, cc)
        return remote(src, ubuf.at[urow(y, cc), ucol(k)], u_own_s.at[at_sem], u_own_r.at[at_sem], ynb[d])

    def u_own_wait(k, d, cc):
        ref = ubuf.at[urow(y, cc), ucol(k)]
        return remote(ref, ref, u_own_s.at[k, d, cc], u_own_r.at[k, d, cc], ynb[d])

    def u_fwd(k, d):
        yy = (y + 3) % 4 if d == 0 else (y + 1) % 4
        ref = ubuf.at[urow(yy, d), ucol(k)]
        return remote(ref, ref, u_fwd_s.at[k, d], u_fwd_r.at[k, d], ynb[d])

    def issue_own(k):
        for d in range(2):
            u_own(k, d, True).start()
        u_sib(k).wait_recv()
        for d in range(2):
            u_own(k, d, False).start()

    def y_stage(k):
        for d in range(2):
            u_own_wait(k, d, d).wait_recv()
            u_fwd(k, d).start()

        @pl.when(k + 2 < 2 * subs)
        def _():
            issue_own(k + 2)

    def u_ready(k):
        u_local(k).wait()
        for d in range(2):
            u_own_wait(k, d, 1 - d).wait_recv()
        for d in range(2):
            u_fwd(k, d).wait_recv()

    def wref(hi, first, count, side, p):
        return wbuf.at[aligned(hi * blk + first, count), aligned(side * quarter + p * cw, cw)]

    def w_own(p, d):
        return remote(wref(zh, 0, blk, 0, p), wref(zh, 0, blk, 1, p), w_own_s.at[p, d], w_own_r.at[p, d], znb[d])

    def w_fwd(p, d):
        hi = zside[1 - d]
        return remote(
            wref(hi, d * half, half, 1, p), wref(hi, d * half, half, 0, p), w_fwd_s.at[p, d], w_fwd_r.at[p, d], znb[d]
        )

    def clip_weights(t, _):
        i, p = t % 4, t // 4
        for j in range(cw // TILE):
            bound = levels[i, p * (cw // TILE) + j].astype(jnp.float32) * clip_step
            place = (aligned(i * TILE, TILE), aligned(p * cw + j * TILE, TILE))
            noisy = weight[place].astype(jnp.float32) + noise[place].astype(jnp.float32)
            wbuf[aligned(zh * blk + i * TILE, TILE), aligned(p * cw + j * TILE, TILE)] = jnp.minimum(
                jnp.maximum(noisy, -bound), bound
            ).astype(jnp.bfloat16)
        return 0

    def ccol(hi):
        return aligned(hi * blk, blk)

    crows = aligned(c * rows, rows, 16)
    c_local = pltpu.make_async_copy(picked.at[zh], cbuf.at[crows, ccol(zh)], c_loc.at[0])
    c_opp = remote(picked.at[1 - zh], cbuf.at[crows, ccol(zh)], c_opp_s.at[0], c_opp_r.at[0], opp)
    c_sib = remote(cbuf.at[crows], cbuf.at[crows], c_sib_s.at[0], c_sib_r.at[0], sib)

    def turn(t, _):
        place = aligned(t * TILE, TILE)
        ctbuf[:, place] = cbuf[place, :].T
        return 0

    def tile_grad(hi, k, n):
        cols = aligned((k % 2) * quarter + (k // 2) * cw + n * 256, 256)
        return jnp.dot(ctbuf[aligned(hi * blk, blk), :], ubuf[:, cols], preferred_element_type=jnp.float32)

    def g_half(s, d):
        return remote(
            gopp.at[s, pl.ds(d * half, half)], ghalf.at[d, s], g_half_s.at[s, d], g_half_r.at[s, d], znb[d]
        )

    def g_full(s, d):
        return remote(gside.at[d, s], gfull.at[d, s], g_full_s.at[s, d], g_full_r.at[s, d], znb[d])

    def grad_same(s):
        u_ready(2 * s)

        def body(n, _):
            gself[:, aligned(s * cw + n * 256, 256)] = tile_grad(zh, 2 * s, n)
            gopp[s, :, aligned(n * 256, 256)] = tile_grad(1 - zh, 2 * s, n).astype(jnp.bfloat16)
            return 0

        lax.fori_loop(0, cw // 256, body, 0)
        for d in range(2):
            g_half(s, d).start()

    def grad_side(s):
        u_ready(2 * s + 1)

        def body(n, _):
            for d in range(2):
                gside[d, s, :, aligned(n * 256, 256)] = tile_grad(zside[d], 2 * s + 1, n).astype(jnp.bfloat16)
            return 0

        lax.fori_loop(0, cw // 256, body, 0)

    def combine(s):
        for d in range(2):
            g_half(s, d).wait_recv()
            place = pl.ds(d * half, half)
            gside[d, s, place] = (
                gside[d, s, place].astype(jnp.float32) + ghalf[d, s].astype(jnp.float32)
            ).astype(jnp.bfloat16)
            g_full(s, d).start()

    def master_copy(s):
        place = aligned(s * cw, cw)
        return pltpu.make_async_copy(gself.at[:, place], master.at[:, place], m_out.at[s])

    def finish(s):
        for d in range(2):
            g_full(s, d).wait_recv()

        def body(i, _):
            line = aligned(i * TILE, TILE)
            for j in range(cw // TILE):
                bound = levels[i, s * (cw // TILE) + j].astype(jnp.float32) * clip_step
                place = (line, aligned(s * cw + j * TILE, TILE))
                noisy = weight[place].astype(jnp.float32) + noise[place].astype(jnp.float32)
                inner = pl.ds(j * TILE, TILE)
                total = gself[place] + gfull[0, s, line, inner].astype(jnp.float32)
                total = total + gfull[1, s, line, inner].astype(jnp.float32)
                gself[place] = jnp.where(jnp.abs(noisy) <= bound, total, 0.0)
            return 0

        lax.fori_loop(0, blk // TILE, body, 0)
        master_copy(s).start()

    def w_ready(p):
        for d in range(2):
            w_fwd(p, d).wait_recv()

    def tile_branch(first, n, s):
        total = None
        for side in range(2):
            cols = aligned(side * quarter + s * cw, cw)
            term = lax.dot_general(
                ubuf[aligned(first, rows, 16), cols],
                wbuf[aligned(n * 256, 256), cols],
                (((1,), (1,)), ((), ())),
                preferred_element_type=jnp.float32,
            )
            total = term if total is None else total + term
        return total

    def branch_part(s):
        w_ready(s)

        def body(t, _):
            first, n = (t // 4) * rows, t % 4
            place = (aligned(first, rows, 16), aligned(n * 256, 256))
            acc[place] += tile_branch(first, n, s)
            return 0

        lax.fori_loop(0, 2 * (feats // 256), body, 0)

    def b_sib(n):
        cols = aligned(n * 256, 256)
        return remote(bsend.at[:, cols], brecv.at[:, cols], b_sib_s.at[n], b_sib_r.at[n], sib)

    def b_out(n, j):
        yt = (y + j) % 4
        return remote(
            bout.at[aligned(yt * tok, tok, 16), aligned(n * 256, 256)],
            passed.at[:, aligned(y * feats + n * 256, 256)],
            b_out_s.at[n, j], b_out_r.at[n, j], at(x + 3, yt, z, c),
        )

    def branch_last(s):
        w_ready(s)

        def theirs(n, _):
            cols = aligned(n * 256, 256)
            bsend[:, cols] = (
                acc[aligned(oc * rows, rows, 16), cols] + tile_branch(oc * rows, n, s)
            ).astype(jnp.bfloat16)
            b_sib(n).start()
            return 0

        lax.fori_loop(0, feats // 256, theirs, 0)

        def ours(n, _):
            cols = aligned(n * 256, 256)
            total = acc[aligned(c * rows, rows, 16), cols] + tile_branch(c * rows, n, s)
            b_sib(n).wait_recv()
            bout[:, cols] = (total + brecv[:, cols].astype(jnp.float32)).astype(jnp.bfloat16)
            for j in range(4):
                b_out(n, j).start()
            return 0

        lax.fori_loop(0, feats // 256, ours, 0)

    chunks = 2 * subs
    c_local.start()

    def start_local(k, _):
        u_local(k).start()
        return 0

    lax.fori_loop(0, chunks, start_local, 0)
    pl.semaphore_wait(barrier, len(greet))
    c_opp.start()

    def start_sib(k, _):
        u_sib(k).start()
        return 0

    lax.fori_loop(0, chunks, start_sib, 0)
    for k in range(2):
        issue_own(k)
    lax.fori_loop(0, 16, clip_weights, 0)
    for p in range(2):
        for d in range(2):
            w_own(p, d).start()
    acc[...] = jnp.zeros_like(acc)
    c_local.wait()
    c_opp.wait_recv()
    c_sib.start()

    def pair(s, _):
        k = 2 * s
        y_stage(k)

        @pl.when(s == 1)
        def _():
            for d in range(2):
                w_own(3, d).start()

        @pl.when((s == 1) | (s == 2))
        def _():
            for d in range(2):
                w_own_wait = w_own(k - 2, d)
                w_own_wait.wait_recv()
                w_fwd(k - 2, d).start()

        @pl.when(s >= 1)
        def _():
            grad_side(s - 1)

        @pl.when(s >= 2)
        def _():
            combine(s - 2)

        y_stage(k + 1)

        @pl.when(s == 0)
        def _():
            for d in range(2):
                w_own(2, d).start()
            c_sib.wait_recv()
            lax.fori_loop(0, (2 * rows) // TILE, turn, 0)

        @pl.when((s == 1) | (s == 2))
        def _():
            for d in range(2):
                w_own(k - 1, d).wait_recv()
                w_fwd(k - 1, d).start()

        grad_same(s)

        @pl.when(s >= 1)
        def _():
            branch_part(s - 1)

        return 0

    lax.fori_loop(0, subs, pair, 0)
    grad_side(subs - 1)
    combine(subs - 2)
    branch_last(subs - 1)
    finish(0)
    finish(1)
    combine(subs - 1)
    finish(2)
    finish(3)

    c_opp.wait_send()
    c_sib.wait_send()

    def drain_u(k, _):
        u_sib(k).wait_send()
        for d in range(2):
            for cc in range(2):
                u_own_wait(k, d, cc).wait_send()
            u_fwd(k, d).wait_send()
        return 0

    lax.fori_loop(0, chunks, drain_u, 0)

    def drain(s, _):
        for d in range(2):
            w_own(s, d).wait_send()
            w_fwd(s, d).wait_send()
            g_half(s, d).wait_send()
            g_full(s, d).wait_send()
        b_sib(s).wait_send()
        for j in range(4):
            b_out(s, j).wait()
        master_copy(s).wait()
        return 0

    lax.fori_loop(0, subs, drain, 0)


def relay_call(up, picked, weight, noise, levels):
    tok, width = up.shape
    blk, quarter = weight.shape
    rows = 4 * tok
    brick, feats = 2 * rows, 2 * blk
    span = 2 * quarter
    cw = quarter // 4
    bf, f32 = jnp.bfloat16, jnp.float32
    dma = pltpu.SemaphoreType.DMA
    sems = [
        (8,), (8,), (8,), (8, 2, 2), (8, 2, 2), (8, 2), (8, 2),
        (1,), (1,), (1,), (1,), (1,),
        (4, 2), (4, 2), (4, 2), (4, 2),
        (4, 2), (4, 2), (4, 2), (4, 2),
        (4,), (4,), (4, 4), (4, 4), (4,),
    ]
    flops = 2 * 2 * brick * feats * span
    return pl.pallas_call(
        relay_kernel,
        out_shape=(jax.ShapeDtypeStruct((blk, quarter), f32), jax.ShapeDtypeStruct((tok, 4 * feats), bf)),
        in_specs=[
            pl.BlockSpec(memory_space=pl.ANY),
            pl.BlockSpec(memory_space=pl.ANY),
            pl.BlockSpec(memory_space=pltpu.VMEM),
            pl.BlockSpec(memory_space=pltpu.VMEM),
            pl.BlockSpec(memory_space=pltpu.SMEM),
        ],
        out_specs=(pl.BlockSpec(memory_space=pl.ANY), pl.BlockSpec(memory_space=pl.ANY)),
        scratch_shapes=[
            pltpu.VMEM((brick, span), bf),
            pltpu.VMEM((feats, span), bf),
            pltpu.VMEM((brick, feats), bf),
            pltpu.VMEM((feats, brick), bf),
            pltpu.VMEM((brick, feats), f32),
            pltpu.VMEM((blk, quarter), f32),
            pltpu.VMEM((4, blk, cw), bf),
            pltpu.VMEM((2, 4, blk, cw), bf),
            pltpu.VMEM((2, 4, blk // 2, cw), bf),
            pltpu.VMEM((2, 4, blk, cw), bf),
            pltpu.VMEM((rows, feats), bf),
            pltpu.VMEM((rows, feats), bf),
            pltpu.VMEM((rows, feats), bf),
        ]
        + [dma(shape) for shape in sems],
        compiler_params=pltpu.CompilerParams(
            collective_id=0, has_side_effects=True, vmem_limit_bytes=63 * 1024 * 1024
        ),
        cost_estimate=pl.CostEstimate(flops=flops, bytes_accessed=32 * 1024 * 1024, transcendentals=0),
        name="relay",
    )(up, picked, weight, noise, levels)


def local(upstream, saved_input, weight, weight_noise, levels, plan):
    section = lax.axis_index("pipe")
    tok = upstream.shape[1]
    blk = weight.shape[1]
    total_tokens = tok * lax.axis_size("tp") * lax.axis_size("dp")
    chosen = lax.dynamic_index_in_dim(saved_input[0], plan[section], 0, keepdims=False)
    picked = chosen.reshape(4, 2, tok, blk).transpose(1, 0, 2, 3).reshape(2, 4 * tok, blk)
    grad, arrived = relay_call(upstream[0], picked, weight[0], weight_noise[0], levels[0])
    master = grad * (1.0 / jnp.sqrt(jnp.float32(total_tokens)))
    last = section == lax.axis_size("pipe") - 1
    passed = jnp.where(last, jnp.zeros_like(arrived), arrived)
    return (master[None], passed[None])


def solution(mesh):
    placed = (
        P("pipe", ("dp", "tp"), None),
        P("pipe", None, "dp", "tp"),
        P("pipe", "tp", "dp"),
        P("pipe", "tp", "dp"),
        P("pipe", "tp", "dp"),
        P(),
    )
    return jax.shard_map(
        local,
        mesh=mesh,
        in_specs=placed,
        out_specs=(P("pipe", "tp", "dp"), P("pipe", ("dp", "tp"), None)),
        check_vma=False,
    )
```

```python
import jax
import jax.numpy as jnp
from jax import lax
from jax.experimental import pallas as pl
from jax.experimental.pallas import tpu as pltpu
from jax.sharding import PartitionSpec as P

clip_step = 0.006
MESH = pl.DeviceIdType.MESH
TILE = 128


def aligned(start, size, step=128):
    return pl.ds(pl.multiple_of(start, step), size)


def relay_kernel(
    up, saved, weight_in, noise_in, levels, plan,
    master, passed,
    ubuf, wbuf, cbuf, ctbuf, acc, gbuf, ghalf, gfull, ready, bsend, brecv, bout, weight, noise,
    u_loc, u_sib_s, u_sib_r, u_own_s, u_own_r, u_fwd_s, u_fwd_r,
    c_loc, c_opp_s, c_opp_r, c_sib_s, c_sib_r,
    w_loc, w_own_s, w_own_r, w_fwd_s, w_fwd_r,
    g_half_s, g_half_r, g_full_s, g_full_r,
    b_sib_s, b_sib_r, b_out_s, b_out_r, m_out,
):
    tok = up.shape[0]
    rows = tok * 4
    near, far = 3 * tok, tok
    quarter = weight.shape[1]
    blk = weight.shape[0]
    half = blk // 2
    subs = 4
    chunks = 2 * subs
    cw = quarter // subs
    tiles = cw // TILE
    feats = 2 * blk
    ahead = 4

    x = lax.axis_index("pipe")
    tp = lax.axis_index("tp")
    dp = lax.axis_index("dp")
    y, zh = tp // 2, tp % 2
    zl, c = dp // 2, dp % 2
    z = 2 * zh + zl
    oc = 1 - c

    def at(xx, yy, zz, cc):
        xx, yy, zz = xx % 4, yy % 4, zz % 4
        return (xx, yy * 2 + zz // 2, (zz % 2) * 2 + cc)

    sib = at(x, y, z, oc)
    opp = at(x, y, z + 2, c)
    ynb = (at(x, y + 1, z, c), at(x, y + 3, z, c))
    znb = (at(x, y, z + 1, c), at(x, y, z + 3, c))
    zp = (zh + zl) % 2
    zside = (zp, 1 - zp)

    barrier = pltpu.get_barrier_semaphore()
    greet = [sib, opp, *ynb, *znb] + [at(x + 1, y + j, z, c) for j in range(4)]
    for one in greet:
        pl.semaphore_signal(barrier, inc=1, device_id=one, device_id_type=MESH)

    def remote(src, dst, s, r, to):
        return pltpu.make_async_remote_copy(
            src_ref=src, dst_ref=dst, send_sem=s, recv_sem=r, device_id=to, device_id_type=MESH
        )

    def each(count, body):
        def one(i, _):
            body(i)
            return 0

        lax.fori_loop(0, count, one, 0)

    def near_rows(cc):
        return aligned(cc * near, near, 16)

    def far_rows(cc):
        return aligned(2 * near + cc * far, far, 16)

    def row(slot, cc):
        return aligned(cc * near + slot * tok, tok, 16)

    def ucol(k):
        return aligned((k % 2) * quarter + (k // 2) * cw, cw)

    def hcol(k, cc):
        return aligned(((zl + k) % 2) * (2 * quarter) + cc * quarter + (k // 2) * cw, cw)

    def u_local(k):
        return pltpu.make_async_copy(up.at[:, hcol(k, c)], ubuf.at[row(0, c), ucol(k)], u_loc.at[k])

    def u_sib(k):
        return remote(up.at[:, hcol(k, oc)], ubuf.at[row(0, c), ucol(k)], u_sib_s.at[k], u_sib_r.at[k], sib)

    def u_own(k, d, mine):
        cc = c if mine else oc
        src = up.at[:, hcol(k, c)] if mine else ubuf.at[row(0, oc), ucol(k)]
        return remote(src, ubuf.at[row(2 - d, cc), ucol(k)], u_own_s.at[k, d, cc], u_own_r.at[k, d, cc], ynb[d])

    def u_own_wait(k, d, cc):
        ref = ubuf.at[row(2 - d, cc), ucol(k)]
        return remote(ref, ref, u_own_s.at[k, d, cc], u_own_r.at[k, d, cc], ynb[d])

    def u_fwd(k, d):
        return remote(
            ubuf.at[row(2 - d, d), ucol(k)], ubuf.at[far_rows(d), ucol(k)], u_fwd_s.at[k, d], u_fwd_r.at[k, d], ynb[d]
        )

    def own_mine(k):
        for d in range(2):
            u_own(k, d, True).start()

    def own_theirs(k):
        u_sib(k).wait_recv()
        for d in range(2):
            u_own(k, d, False).start()

    def pass_on(k):
        for d in range(2):
            u_fwd(k, d).start()

    def w_load(p):
        place = aligned(p * cw, cw)
        return [
            pltpu.make_async_copy(weight_in.at[:, place], weight.at[:, place], w_loc.at[p, 0]),
            pltpu.make_async_copy(noise_in.at[:, place], noise.at[:, place], w_loc.at[p, 1]),
        ]

    def wref(hi, first, count, side, p):
        return wbuf.at[aligned(hi * blk + first, count), aligned(side * quarter + p * cw, cw)]

    def w_own(p, d):
        return remote(wref(zh, 0, blk, 0, p), wref(zh, 0, blk, 1, p), w_own_s.at[p, d], w_own_r.at[p, d], znb[d])

    def w_fwd(p, d):
        hi = zside[1 - d]
        return remote(
            wref(hi, d * half, half, 1, p), wref(hi, d * half, half, 0, p), w_fwd_s.at[p, d], w_fwd_r.at[p, d], znb[d]
        )

    def w_pass_on(p):
        for d in range(2):
            w_own(p, d).wait_recv()
            w_fwd(p, d).start()

    def clip_weights(p):
        for one in w_load(p):
            one.wait()

        def body(i):
            for j in range(tiles):
                bound = levels[i, p * tiles + j].astype(jnp.float32) * clip_step
                place = (aligned(i * TILE, TILE), aligned(p * cw + j * TILE, TILE))
                noisy = weight[place].astype(jnp.float32) + noise[place].astype(jnp.float32)
                wbuf[aligned(zh * blk + i * TILE, TILE), aligned(p * cw + j * TILE, TILE)] = jnp.minimum(
                    jnp.maximum(noisy, -bound), bound
                ).astype(jnp.bfloat16)

        each(blk // TILE, body)

    def c_load(t):
        slot, other = t // 2, t % 2
        rel = (0, 1, 3, 2)[slot]
        place = (pl.ds(slot * tok, tok), pl.ds(other * blk, blk))
        src = ((y + rel) % 4, (zh + other) % 2)
        return [
            pltpu.make_async_copy(saved.at[(0, *src)], bsend.at[place], c_loc.at[t, 0]),
            pltpu.make_async_copy(saved.at[(1, *src)], bout.at[place], c_loc.at[t, 1]),
        ]

    def ccol(hi):
        return aligned(hi * blk, blk)

    def c_opp(part):
        src = (pl.ds(0, near), pl.ds(near, far))[part]
        dst = (near_rows(c), far_rows(c))[part]
        return remote(
            bout.at[src, pl.ds(blk, blk)], cbuf.at[dst, ccol(zh)], c_opp_s.at[part], c_opp_r.at[part], opp
        )

    def c_sib(part):
        ref = cbuf.at[(near_rows(c), far_rows(c))[part]]
        return remote(ref, ref, c_sib_s.at[part], c_sib_r.at[part], sib)

    def pick_batch():
        for t in range(8):
            for one in c_load(t):
                one.wait()
        second = plan[x].astype(jnp.float32)
        first = 1.0 - second

        def picked(place):
            return (
                bsend[place].astype(jnp.float32) * first + bout[place].astype(jnp.float32) * second
            ).astype(jnp.bfloat16)

        for slot in range(4):
            begin = c * near + slot * tok if slot < 3 else 2 * near + c * far

            def body(i):
                src = aligned(slot * tok + i * 16, 16, 16)
                cbuf[aligned(begin + i * 16, 16, 16), ccol(zh)] = picked((src, pl.ds(0, blk)))
                other = (src, pl.ds(blk, blk))
                bout[other] = picked(other)

            each(tok // 16, body)

    def turn(t):
        place = aligned(t * TILE, TILE)
        ctbuf[:, place] = cbuf[place, :].T

    def grad_chunk(k):
        for d in range(2):
            u_fwd(k, d).wait_recv()

        def body(t):
            b, n = t // 2, t % 2
            hi = (b + zh + (k % 2) * zl) % 2
            cols = aligned((k % 2) * quarter + (k // 2) * cw + n * 256, 256)
            gbuf[k, b, :, aligned(n * 256, 256)] = jnp.dot(
                ctbuf[aligned(hi * blk, blk), :], ubuf[:, cols], preferred_element_type=jnp.float32
            ).astype(jnp.bfloat16)

        each(4, body)

        @pl.when(k % 2 == 0)
        def _():
            for d in range(2):
                g_half(k // 2, d).start()

    def g_half(s, d):
        return remote(
            gbuf.at[2 * s, 1, pl.ds(d * half, half)], ghalf.at[d, s], g_half_s.at[s, d], g_half_r.at[s, d], znb[d]
        )

    def g_full(s, d):
        return remote(gbuf.at[2 * s + 1, d], gfull.at[d, s], g_full_s.at[s, d], g_full_r.at[s, d], znb[d])

    def combine(s):
        for d in range(2):
            g_half(s, d).wait_recv()
            for i in range(half // 64):
                inner = pl.ds(i * 64, 64)
                place = pl.ds(d * half + i * 64, 64)
                gbuf[2 * s + 1, d, place] = (
                    gbuf[2 * s + 1, d, place].astype(jnp.float32) + ghalf[d, s, inner].astype(jnp.float32)
                ).astype(jnp.bfloat16)
            g_full(s, d).start()

    def master_copy(s):
        return pltpu.make_async_copy(ready.at[s], master.at[:, aligned(s * cw, cw)], m_out.at[s])

    def finish(s):
        for d in range(2):
            g_full(s, d).wait_recv()
        scale = 1.0 / (float(rows) * 8.0) ** 0.5

        def body(i):
            line = aligned(i * TILE, TILE)
            for j in range(tiles):
                bound = levels[i, s * tiles + j].astype(jnp.float32) * clip_step
                place = (line, aligned(s * cw + j * TILE, TILE))
                noisy = weight[place].astype(jnp.float32) + noise[place].astype(jnp.float32)
                inner = pl.ds(j * TILE, TILE)
                total = gbuf[2 * s, 0, line, inner].astype(jnp.float32) + gfull[0, s, line, inner].astype(jnp.float32)
                total = total + gfull[1, s, line, inner].astype(jnp.float32)
                ready[s, line, inner] = jnp.where(jnp.abs(noisy) <= bound, total * scale, 0.0)

        each(blk // TILE, body)
        master_copy(s).start()

    def w_ready(p):
        for d in range(2):
            w_fwd(p, d).wait_recv()

    def tile_branch(place, n, sides):
        total = None
        for cols in sides:
            term = lax.dot_general(
                ubuf[place, cols],
                wbuf[aligned(n * 256, 256), cols],
                (((1,), (1,)), ((), ())),
                preferred_element_type=jnp.float32,
            )
            total = term if total is None else total + term
        return total

    def branch_near(s):
        w_ready(s)
        sides = [aligned(side * quarter + s * cw, cw) for side in range(2)]

        def body(t):
            place, cols = near_rows(t // 4), aligned((t % 4) * 256, 256)
            acc[place, cols] += tile_branch(place, t % 4, sides)

        each(2 * (feats // 256), body)

    def b_sib(part, n):
        place = ((pl.ds(0, near), pl.ds(near, far))[part], aligned(n * 256, 256))
        return remote(bsend.at[place], brecv.at[place], b_sib_s.at[part, n], b_sib_r.at[part, n], sib)

    def b_out(n, slot):
        yt = (y + (0, 1, 3, 2)[slot]) % 4
        return remote(
            bout.at[pl.ds(slot * tok, tok), aligned(n * 256, 256)],
            passed.at[:, aligned(y * feats + n * 256, 256)],
            b_out_s.at[n, slot], b_out_r.at[n, slot], at(x + 3, yt, z, c),
        )

    def branch_send(part, first, count, slots):
        def place(cc):
            return aligned(cc * count, count, 16)

        def theirs(n):
            cols = aligned(n * 256, 256)
            bsend[pl.ds(first, count), cols] = acc[place(oc), cols].astype(jnp.bfloat16)
            b_sib(part, n).start()

        each(feats // 256, theirs)

        def ours(n):
            cols = aligned(n * 256, 256)
            b_sib(part, n).wait_recv()
            total = acc[place(c), cols] + brecv[pl.ds(first, count), cols].astype(jnp.float32)
            bout[pl.ds(first, count), cols] = jnp.where(x == 0, 0.0, total).astype(jnp.bfloat16)
            for slot in slots:
                b_out(n, slot).start()

        each(feats // 256, ours)

    def branch_far():
        whole = pl.ds(2 * near, 2 * far)

        def body(n):
            acc[pl.ds(0, 2 * far), aligned(n * 256, 256)] = tile_branch(
                whole, n, [pl.ds(i * quarter, quarter) for i in range(2)]
            )

        each(feats // 256, body)

    for p in range(subs):
        for one in w_load(p):
            one.start()
    for t in range(8):
        for one in c_load(t):
            one.start()
    each(chunks, lambda k: u_local(k).start())
    each(subs, clip_weights)
    pl.semaphore_wait(barrier, len(greet))
    for k in range(2):
        u_sib(k).start()
        own_mine(k)
    for p in range(2):
        for d in range(2):
            w_own(p, d).start()
    each(chunks - 2, lambda k: u_sib(k + 2).start())
    for k in range(2):
        own_theirs(k)
    pick_batch()
    for part in range(2):
        c_opp(part).start()
    for p in range(2, 4):
        for d in range(2):
            w_own(p, d).start()
    acc[...] = jnp.zeros_like(acc)

    def step(k):
        @pl.when(k < chunks)
        def _():
            for d in range(2):
                u_own_wait(k, d, d).wait_recv()

            @pl.when(k >= ahead - 1)
            def _():
                pass_on(k - (ahead - 1))

            @pl.when(k + 2 < chunks)
            def _():
                own_mine(k + 2)
                own_theirs(k + 2)

            @pl.when(k == chunks - 1)
            def _():
                each(ahead - 1, lambda i: pass_on(chunks - ahead + 1 + i))

            u_local(k).wait()
            for d in range(2):
                u_own_wait(k, d, 1 - d).wait_recv()

        @pl.when(k < 2)
        def _():
            w_pass_on(k)

        @pl.when(k == 3)
        def _():
            for part in range(2):
                c_opp(part).wait_recv()
                c_sib(part).start()
            for part in range(2):
                c_sib(part).wait_recv()
            each((2 * rows) // TILE, turn)

        @pl.when(k >= ahead)
        def _():
            grad_chunk(k - ahead)

        @pl.when((k == 4) | (k == 5))
        def _():
            w_pass_on(k - 2)

        @pl.when((k >= 4) & (k < 8))
        def _():
            branch_near(k - 4)

        @pl.when(k == 7)
        def _():
            for part in range(2):
                c_opp(part).wait_send()
            branch_send(0, 0, near, (0, 1, 2))

        @pl.when((k == 6) | (k == 8))
        def _():
            combine((k - 6) // 2)

    each(chunks + ahead, step)
    branch_far()
    branch_send(1, near, far, (3,))
    combine(2)
    finish(0)
    finish(1)
    combine(3)
    finish(2)
    finish(3)

    for part in range(2):
        c_sib(part).wait_send()

    def drain_u(k):
        u_sib(k).wait_send()
        for d in range(2):
            for cc in range(2):
                u_own_wait(k, d, cc).wait_send()
            u_fwd(k, d).wait_send()

    each(chunks, drain_u)

    def drain(s):
        for d in range(2):
            w_own(s, d).wait_send()
            w_fwd(s, d).wait_send()
            g_half(s, d).wait_send()
            g_full(s, d).wait_send()
        for part in range(2):
            b_sib(part, s).wait_send()
        for slot in range(4):
            b_out(s, slot).wait()
        master_copy(s).wait()

    each(subs, drain)


def relay_call(up, saved, weight, noise, levels, plan):
    tok, width = up.shape
    blk, quarter = weight.shape
    rows = 4 * tok
    brick, feats = 2 * rows, 2 * blk
    span = 2 * quarter
    cw = quarter // 4
    bf, f32 = jnp.bfloat16, jnp.float32
    dma = pltpu.SemaphoreType.DMA
    sems = [
        (8,), (8,), (8,), (8, 2, 2), (8, 2, 2), (8, 2), (8, 2),
        (8, 2), (2,), (2,), (2,), (2,),
        (4, 2), (4, 2), (4, 2), (4, 2), (4, 2),
        (4, 2), (4, 2), (4, 2), (4, 2),
        (2, 4), (2, 4), (4, 4), (4, 4), (4,),
    ]
    flops = 2 * 2 * brick * feats * span
    anywhere = pl.BlockSpec(memory_space=pl.ANY)
    scalars = pl.BlockSpec(memory_space=pltpu.SMEM)
    return pl.pallas_call(
        relay_kernel,
        out_shape=(jax.ShapeDtypeStruct((blk, quarter), f32), jax.ShapeDtypeStruct((tok, 4 * feats), bf)),
        in_specs=[anywhere, anywhere, anywhere, anywhere, scalars, scalars],
        out_specs=(anywhere, anywhere),
        scratch_shapes=[
            pltpu.VMEM((brick, span), bf),
            pltpu.VMEM((feats, span), bf),
            pltpu.VMEM((brick, feats), bf),
            pltpu.VMEM((feats, brick), bf),
            pltpu.VMEM((6 * tok, feats), f32),
            pltpu.VMEM((8, 2, blk, cw), bf),
            pltpu.VMEM((2, 4, blk // 2, cw), bf),
            pltpu.VMEM((2, 4, blk, cw), bf),
            pltpu.VMEM((4, blk, cw), f32),
            pltpu.VMEM((rows, feats), bf),
            pltpu.VMEM((rows, feats), bf),
            pltpu.VMEM((rows, feats), bf),
            pltpu.VMEM((blk, quarter), bf),
            pltpu.VMEM((blk, quarter), bf),
        ]
        + [dma(shape) for shape in sems],
        compiler_params=pltpu.CompilerParams(
            collective_id=0, has_side_effects=True, vmem_limit_bytes=63 * 1024 * 1024
        ),
        cost_estimate=pl.CostEstimate(flops=flops, bytes_accessed=32 * 1024 * 1024, transcendentals=0),
        name="relay",
    )(up, saved, weight, noise, levels, plan)


def hand_over(grad, arrived):
    parts = 8
    pieces = []
    for which, one in enumerate((grad, arrived)):
        many = parts if one.shape[0] % (parts * 16) == 0 else 1
        size = one.shape[0] // many
        pieces += [(which, pl.ds(i * size, size)) for i in range(many)]

    def kernel(grad_in, arrived_in, grad_out, arrived_out, grad_held, arrived_held, load_sem, store_sem):
        routes = ((grad_in, grad_held, grad_out), (arrived_in, arrived_held, arrived_out))
        loads, stores = [], []
        for i, (which, place) in enumerate(pieces):
            src, held, dst = (ref.at[place] for ref in routes[which])
            loads.append(pltpu.make_async_copy(src, held, load_sem.at[i]))
            stores.append(pltpu.make_async_copy(held, dst, store_sem.at[i]))
        for one in loads:
            one.start()
        for load, store in zip(loads, stores):
            load.wait()
            store.start()
        for one in stores:
            one.wait()

    anywhere = pl.BlockSpec(memory_space=pl.ANY)
    return pl.pallas_call(
        kernel,
        out_shape=tuple(jax.ShapeDtypeStruct(one.shape, one.dtype) for one in (grad, arrived)),
        in_specs=[anywhere, anywhere],
        out_specs=(anywhere, anywhere),
        scratch_shapes=[pltpu.VMEM(one.shape, one.dtype) for one in (grad, arrived)]
        + [pltpu.SemaphoreType.DMA((len(pieces),)), pltpu.SemaphoreType.DMA((len(pieces),))],
        compiler_params=pltpu.CompilerParams(vmem_limit_bytes=63 * 1024 * 1024),
        name="hand_over",
    )(grad, arrived)


def local(upstream, saved_input, weight, weight_noise, levels, plan):
    tok = upstream.shape[1]
    blk = weight.shape[1]
    saved = saved_input.reshape(saved_input.shape[1], 4, 2, tok, blk)
    grad, arrived = relay_call(upstream[0], saved, weight[0], weight_noise[0], levels[0], plan)
    master, passed = hand_over(grad, arrived)
    return (master[None], passed[None])


def solution(mesh):
    placed = (
        P("pipe", ("dp", "tp"), None),
        P("pipe", None, "dp", "tp"),
        P("pipe", "tp", "dp"),
        P("pipe", "tp", "dp"),
        P("pipe", "tp", "dp"),
        P(),
    )
    return jax.shard_map(
        local,
        mesh=mesh,
        in_specs=placed,
        out_specs=(P("pipe", "tp", "dp"), P("pipe", ("dp", "tp"), None)),
        check_vma=False,
    )
```

```python
import jax
import jax.numpy as jnp
from jax import lax
from jax.experimental import pallas as pl
from jax.experimental.pallas import tpu as pltpu
from jax.sharding import PartitionSpec as P

clip_step = 0.006
MESH = pl.DeviceIdType.MESH
TILE = 128


def aligned(start, size, step=128):
    return pl.ds(pl.multiple_of(start, step), size)


def relay_kernel(
    up, saved, weight_in, noise_in, levels, plan,
    master, passed,
    ubuf, wbuf, cbuf, ctbuf, acc, gbuf, ghalf, gfull, ready, bsend, brecv, bout, weight, noise,
    u_loc, u_sib_s, u_sib_r, u_own_s, u_own_r, u_fwd_s, u_fwd_r,
    c_loc, c_opp_s, c_opp_r, c_sib_s, c_sib_r,
    w_loc, w_own_s, w_own_r, w_leaf_s, w_leaf_r, w_fwd_s, w_fwd_r, w_off_s, w_off_r,
    g_half_s, g_half_r, g_full_s, g_full_r,
    b_sib_s, b_sib_r, b_out_s, b_out_r, m_out,
):
    tok = up.shape[0]
    rows = tok * 4
    near, far = 3 * tok, tok
    quarter = weight.shape[1]
    blk = weight.shape[0]
    half = blk // 2
    subs = 4
    chunks = 2 * subs
    cw = quarter // subs
    tiles = cw // TILE
    feats = 2 * blk
    ahead = 3

    x = lax.axis_index("pipe")
    tp = lax.axis_index("tp")
    dp = lax.axis_index("dp")
    y, zh = tp // 2, tp % 2
    zl, c = dp // 2, dp % 2
    z = 2 * zh + zl
    oc = 1 - c

    def at(xx, yy, zz, cc):
        xx, yy, zz = xx % 4, yy % 4, zz % 4
        return (xx, yy * 2 + zz // 2, (zz % 2) * 2 + cc)

    sib = at(x, y, z, oc)
    opp = at(x, y, z + 2, c)
    ynb = (at(x, y + 1, z, c), at(x, y + 3, z, c))
    znb = (at(x, y, z + 1, c), at(x, y, z + 3, c))
    zp = (zh + zl) % 2
    zside = (zp, 1 - zp)

    barrier = pltpu.get_barrier_semaphore()
    greet = [sib, opp, *ynb, *znb] + [at(x + 1, y + j, z, c) for j in range(4)]
    for one in greet:
        pl.semaphore_signal(barrier, inc=1, device_id=one, device_id_type=MESH)

    @pl.when(x > 0)
    def _():
        pl.semaphore_signal(barrier, inc=1, device_id=at(0, y, z, c), device_id_type=MESH)

    @pl.when(x == 0)
    def _():
        for plane in range(1, 4):
            for step in (1, 3):
                pl.semaphore_signal(barrier, inc=1, device_id=at(plane, y, z + step, c), device_id_type=MESH)

    greeted = len(greet) + 3 - (x + 3) // 4

    def remote(src, dst, s, r, to):
        return pltpu.make_async_remote_copy(
            src_ref=src, dst_ref=dst, send_sem=s, recv_sem=r, device_id=to, device_id_type=MESH
        )

    def each(count, body):
        def one(i, _):
            body(i)
            return 0

        lax.fori_loop(0, count, one, 0)

    def near_rows(cc):
        return aligned(cc * near, near, 16)

    def far_rows(cc):
        return aligned(2 * near + cc * far, far, 16)

    def row(slot, cc):
        return aligned(cc * near + slot * tok, tok, 16)

    def ucol(k):
        return aligned((k % 2) * quarter + (k // 2) * cw, cw)

    def hcol(k, cc):
        return aligned(((zl + k) % 2) * (2 * quarter) + cc * quarter + (k // 2) * cw, cw)

    def u_local(k):
        return pltpu.make_async_copy(up.at[:, hcol(k, c)], ubuf.at[row(0, c), ucol(k)], u_loc.at[k])

    def u_sib(k):
        return remote(up.at[:, hcol(k, oc)], ubuf.at[row(0, c), ucol(k)], u_sib_s.at[k], u_sib_r.at[k], sib)

    def u_own(k, d, mine):
        cc = c if mine else oc
        src = up.at[:, hcol(k, c)] if mine else ubuf.at[row(0, oc), ucol(k)]
        return remote(src, ubuf.at[row(2 - d, cc), ucol(k)], u_own_s.at[k, d, cc], u_own_r.at[k, d, cc], ynb[d])

    def u_own_wait(k, d, cc):
        ref = ubuf.at[row(2 - d, cc), ucol(k)]
        return remote(ref, ref, u_own_s.at[k, d, cc], u_own_r.at[k, d, cc], ynb[d])

    def u_fwd(k, d):
        return remote(
            ubuf.at[row(2 - d, d), ucol(k)], ubuf.at[far_rows(d), ucol(k)], u_fwd_s.at[k, d], u_fwd_r.at[k, d], ynb[d]
        )

    def own_mine(k):
        for d in range(2):
            u_own(k, d, True).start()

    def own_theirs(k):
        u_sib(k).wait_recv()
        for d in range(2):
            u_own(k, d, False).start()

    def pass_on(k):
        for d in range(2):
            u_fwd(k, d).start()

    def w_load(p):
        place = aligned(p * cw, cw)
        return [
            pltpu.make_async_copy(weight_in.at[:, place], weight.at[:, place], w_loc.at[p, 0]),
            pltpu.make_async_copy(noise_in.at[:, place], noise.at[:, place], w_loc.at[p, 1]),
        ]

    def wref(hi, first, count, side, p):
        return wbuf.at[aligned(hi * blk + first, count), aligned(side * quarter + p * cw, cw)]

    def w_own(p, d):
        return remote(
            wref(zh, d * half, half, 0, p), wref(zh, d * half, half, 1, p), w_own_s.at[p, d], w_own_r.at[p, d], znb[d]
        )

    def w_leaf(p, d):
        first = (1 - d) * half
        return remote(
            wref(zh, first, half, 0, p), wref(zh, first, half, 1, p), w_leaf_s.at[p, d], w_leaf_r.at[p, d], znb[d]
        )

    def held(plane, d, u):
        i = ((plane - 1) * 2 + d) * 2 + u
        return wbuf.at[aligned((i // 8) * half, half), aligned((i % 8) * cw, cw)]

    def w_off(d, u):
        to = at(0, y, z + 1 + 2 * d, c)
        return remote(
            wref(zh, (1 - d) * half, half, 0, u + 2), held(x, d, u), w_leaf_s.at[u + 2, d], w_off_r.at[x - 1, d, u], to
        )

    def w_back(plane, d, u):
        dst = wref(zside[1 - d], (1 - d) * half, half, 1, u + 2)
        return remote(
            held(plane, d, u), dst, w_off_s.at[plane - 1, d, u], w_leaf_r.at[u + 2, d], at(plane, y, z, c)
        )

    def w_off_wait(plane, d, u):
        ref = held(plane, d, u)
        return remote(ref, ref, w_off_s.at[plane - 1, d, u], w_off_r.at[plane - 1, d, u], sib)

    def w_fwd(p, d):
        hi = zside[1 - d]
        return remote(
            wref(hi, d * half, half, 1, p), wref(hi, d * half, half, 0, p), w_fwd_s.at[p, d], w_fwd_r.at[p, d], znb[d]
        )

    def w_pass_on(p):
        for d in range(2):
            w_own(p, d).wait_recv()
            w_fwd(p, d).start()

    def clip_weights(p):
        for one in w_load(p):
            one.wait()

        @pl.when(x > 0)
        def _():
            clip_columns(p)

    def clip_columns(p):
        def body(i):
            for j in range(tiles):
                bound = levels[i, p * tiles + j].astype(jnp.float32) * clip_step
                place = (aligned(i * TILE, TILE), aligned(p * cw + j * TILE, TILE))
                noisy = weight[place].astype(jnp.float32) + noise[place].astype(jnp.float32)
                wbuf[aligned(zh * blk + i * TILE, TILE), aligned(p * cw + j * TILE, TILE)] = jnp.minimum(
                    jnp.maximum(noisy, -bound), bound
                ).astype(jnp.bfloat16)

        each(blk // TILE, body)

    def c_load(t):
        slot, other = t // 2, t % 2
        rel = (0, 1, 3, 2)[slot]
        place = (pl.ds(slot * tok, tok), pl.ds(other * blk, blk))
        src = ((y + rel) % 4, (zh + other) % 2)
        return [
            pltpu.make_async_copy(saved.at[(0, *src)], bsend.at[place], c_loc.at[t, 0]),
            pltpu.make_async_copy(saved.at[(1, *src)], bout.at[place], c_loc.at[t, 1]),
        ]

    def ccol(hi):
        return aligned(hi * blk, blk)

    def c_opp(part):
        src = (pl.ds(0, near), pl.ds(near, far))[part]
        dst = (near_rows(c), far_rows(c))[part]
        return remote(
            bout.at[src, pl.ds(blk, blk)], cbuf.at[dst, ccol(zh)], c_opp_s.at[part], c_opp_r.at[part], opp
        )

    def c_sib(part):
        ref = cbuf.at[(near_rows(c), far_rows(c))[part]]
        return remote(ref, ref, c_sib_s.at[part], c_sib_r.at[part], sib)

    def pick_batch():
        for t in range(8):
            for one in c_load(t):
                one.wait()
        second = plan[x].astype(jnp.float32)
        first = 1.0 - second

        def picked(place):
            return (
                bsend[place].astype(jnp.float32) * first + bout[place].astype(jnp.float32) * second
            ).astype(jnp.bfloat16)

        for slot in range(4):
            begin = c * near + slot * tok if slot < 3 else 2 * near + c * far

            def body(i):
                src = aligned(slot * tok + i * 16, 16, 16)
                cbuf[aligned(begin + i * 16, 16, 16), ccol(zh)] = picked((src, pl.ds(0, blk)))
                other = (src, pl.ds(blk, blk))
                bout[other] = picked(other)

            each(tok // 16, body)

    def turn(t):
        place = aligned(t * TILE, TILE)
        ctbuf[:, place] = cbuf[place, :].T

    def grad_chunk(k):
        for d in range(2):
            u_fwd(k, d).wait_recv()

        def body(t):
            b, n = t // 2, t % 2
            hi = (b + zh + (k % 2) * zl) % 2
            cols = aligned((k % 2) * quarter + (k // 2) * cw + n * 256, 256)
            gbuf[k, b, :, aligned(n * 256, 256)] = jnp.dot(
                ctbuf[aligned(hi * blk, blk), :], ubuf[:, cols], preferred_element_type=jnp.float32
            ).astype(jnp.bfloat16)

        each(4, body)

        @pl.when(k % 2 == 0)
        def _():
            for d in range(2):
                g_half(k // 2, d).start()

    def g_half(s, d):
        return remote(
            gbuf.at[2 * s, 1, pl.ds(d * half, half)], ghalf.at[d, s], g_half_s.at[s, d], g_half_r.at[s, d], znb[d]
        )

    def g_full(s, d):
        return remote(gbuf.at[2 * s + 1, d], gfull.at[d, s], g_full_s.at[s, d], g_full_r.at[s, d], znb[d])

    def combine(s):
        for d in range(2):
            g_half(s, d).wait_recv()
            for i in range(half // 64):
                inner = pl.ds(i * 64, 64)
                place = pl.ds(d * half + i * 64, 64)
                gbuf[2 * s + 1, d, place] = (
                    gbuf[2 * s + 1, d, place].astype(jnp.float32) + ghalf[d, s, inner].astype(jnp.float32)
                ).astype(jnp.bfloat16)
            g_full(s, d).start()

    def master_copy(s):
        return pltpu.make_async_copy(ready.at[s], master.at[:, aligned(s * cw, cw)], m_out.at[s])

    def finish(s):
        for d in range(2):
            g_full(s, d).wait_recv()
        scale = 1.0 / (float(rows) * 8.0) ** 0.5

        def body(i):
            line = aligned(i * TILE, TILE)
            for j in range(tiles):
                bound = levels[i, s * tiles + j].astype(jnp.float32) * clip_step
                place = (line, aligned(s * cw + j * TILE, TILE))
                noisy = weight[place].astype(jnp.float32) + noise[place].astype(jnp.float32)
                inner = pl.ds(j * TILE, TILE)
                total = gbuf[2 * s, 0, line, inner].astype(jnp.float32) + gfull[0, s, line, inner].astype(jnp.float32)
                total = total + gfull[1, s, line, inner].astype(jnp.float32)
                ready[s, line, inner] = jnp.where(jnp.abs(noisy) <= bound, total * scale, 0.0)

        each(blk // TILE, body)
        master_copy(s).start()

    def w_ready(p):
        for d in range(2):
            w_leaf(p, d).wait_recv()
            w_fwd(p, d).wait_recv()

    def tile_branch(place, n, sides):
        total = None
        for cols in sides:
            term = lax.dot_general(
                ubuf[place, cols],
                wbuf[aligned(n * 256, 256), cols],
                (((1,), (1,)), ((), ())),
                preferred_element_type=jnp.float32,
            )
            total = term if total is None else total + term
        return total

    def branch_near(s):
        w_ready(s)
        sides = [aligned(side * quarter + s * cw, cw) for side in range(2)]

        def body(t):
            place, cols = near_rows(t // 4), aligned((t % 4) * 256, 256)
            acc[place, cols] += tile_branch(place, t % 4, sides)

        each(2 * (feats // 256), body)

    def b_sib(part, n):
        place = ((pl.ds(0, near), pl.ds(near, far))[part], aligned(n * 256, 256))
        return remote(bsend.at[place], brecv.at[place], b_sib_s.at[part, n], b_sib_r.at[part, n], sib)

    def b_out(n, slot):
        yt = (y + (0, 1, 3, 2)[slot]) % 4
        return remote(
            bout.at[pl.ds(slot * tok, tok), aligned(n * 256, 256)],
            passed.at[:, aligned(y * feats + n * 256, 256)],
            b_out_s.at[n, slot], b_out_r.at[n, slot], at(x + 3, yt, z, c),
        )

    def branch_send(part, first, count, slots):
        def place(cc):
            return aligned(cc * count, count, 16)

        def theirs(n):
            cols = aligned(n * 256, 256)
            bsend[pl.ds(first, count), cols] = acc[place(oc), cols].astype(jnp.bfloat16)
            b_sib(part, n).start()

        def ours(n):
            cols = aligned(n * 256, 256)
            b_sib(part, n).wait_recv()
            total = acc[place(c), cols] + brecv[pl.ds(first, count), cols].astype(jnp.float32)
            bout[pl.ds(first, count), cols] = total.astype(jnp.bfloat16)

        def send(n):
            for slot in slots:
                b_out(n, slot).start()

        @pl.when(x > 0)
        def _():
            each(feats // 256, theirs)

            def both(n):
                ours(n)
                send(n)

            each(feats // 256, both)

        @pl.when(x == 0)
        def _():
            bout[pl.ds(first, count), :] = jnp.zeros((count, feats), jnp.bfloat16)
            each(feats // 256, send)

    def branch_far():
        whole = pl.ds(2 * near, 2 * far)

        def body(n):
            acc[pl.ds(0, 2 * far), aligned(n * 256, 256)] = tile_branch(
                whole, n, [pl.ds(i * quarter, quarter) for i in range(2)]
            )

        each(feats // 256, body)

    for p in range(subs):
        for one in w_load(p):
            one.start()
    for t in range(8):
        for one in c_load(t):
            one.start()
    each(chunks, lambda k: u_local(k).start())
    each(subs, clip_weights)
    pl.semaphore_wait(barrier, greeted)
    for k in range(2):
        u_sib(k).start()
        own_mine(k)

    pick_batch()
    for part in range(2):
        c_opp(part).start()

    @pl.when(x > 0)
    def _():
        for u in range(2):
            for d in range(2):
                w_off(d, u).start()
        for d in range(2):
            w_own(0, d).start()
            w_leaf(0, d).start()

    each(chunks - 2, lambda k: u_sib(k + 2).start())
    for k in range(2):
        own_theirs(k)
    acc[...] = jnp.zeros_like(acc)

    def step(k):
        @pl.when(k < chunks)
        def _():
            for d in range(2):
                u_own_wait(k, d, d).wait_recv()

            @pl.when(k >= ahead - 1)
            def _():
                pass_on(k - (ahead - 1))

            @pl.when(k + 2 < chunks)
            def _():
                own_mine(k + 2)
                own_theirs(k + 2)

            @pl.when(k == chunks - 1)
            def _():
                each(ahead - 1, lambda i: pass_on(chunks - ahead + 1 + i))

            u_local(k).wait()
            for d in range(2):
                u_own_wait(k, d, 1 - d).wait_recv()

        @pl.when((x == 0) & ((k == 2) | (k == 4)))
        def _():
            u = (k - 2) // 2
            for plane in (1, 3, 2):
                for d in range(2):
                    w_off_wait(plane, d, u).wait_recv()
                    w_back(plane, d, u).start()

        @pl.when((x > 0) & (k == 1))
        def _():
            w_pass_on(0)

        @pl.when((x > 0) & (k == 2))
        def _():
            for d in range(2):
                w_own(1, d).start()
                w_leaf(1, d).start()
                w_own(2, d).start()

        @pl.when((x > 0) & (k == 3))
        def _():
            for d in range(2):
                w_own(3, d).start()

        @pl.when(k == 3)
        def _():
            for part in range(2):
                c_opp(part).wait_recv()
                c_sib(part).start()
            for part in range(2):
                c_sib(part).wait_recv()
            each((2 * rows) // TILE, turn)

        @pl.when((x > 0) & (k == 4))
        def _():
            w_pass_on(1)
            w_pass_on(2)

        @pl.when((x > 0) & (k == 5))
        def _():
            w_pass_on(3)

        @pl.when((k >= ahead) & (k != 7))
        def _():
            grad_chunk(k - ahead)

        @pl.when((x > 0) & (k >= 4) & (k < 8))
        def _():
            branch_near(k - 4)

        @pl.when((k == 5) | (k == 7) | (k == 9))
        def _():
            combine((k - 5) // 2)

        @pl.when(k == 7)
        def _():
            for part in range(2):
                c_opp(part).wait_send()
            branch_send(0, 0, near, (0, 1, 2))
            grad_chunk(k - ahead)

    each(chunks + ahead, step)

    @pl.when(x > 0)
    def _():
        branch_far()

    branch_send(1, near, far, (3,))
    combine(3)
    finish(0)
    finish(1)
    finish(2)
    finish(3)

    for part in range(2):
        c_sib(part).wait_send()

    def drain_u(k):
        u_sib(k).wait_send()
        for d in range(2):
            for cc in range(2):
                u_own_wait(k, d, cc).wait_send()
            u_fwd(k, d).wait_send()

    each(chunks, drain_u)

    def drain(s):
        for d in range(2):
            g_half(s, d).wait_send()
            g_full(s, d).wait_send()

        @pl.when(x > 0)
        def _():
            for d in range(2):
                w_own(s, d).wait_send()
                w_leaf(s, d).wait_send()
                w_fwd(s, d).wait_send()
            for part in range(2):
                b_sib(part, s).wait_send()

        for slot in range(4):
            b_out(s, slot).wait()
        master_copy(s).wait()

    each(subs, drain)

    @pl.when(x == 0)
    def _():
        for plane in range(1, 4):
            for d in range(2):
                for u in range(2):
                    w_back(plane, d, u).wait_send()


def relay_call(up, saved, weight, noise, levels, plan):
    tok, width = up.shape
    blk, quarter = weight.shape
    rows = 4 * tok
    brick, feats = 2 * rows, 2 * blk
    span = 2 * quarter
    cw = quarter // 4
    bf, f32 = jnp.bfloat16, jnp.float32
    dma = pltpu.SemaphoreType.DMA
    sems = [
        (8,), (8,), (8,), (8, 2, 2), (8, 2, 2), (8, 2), (8, 2),
        (8, 2), (2,), (2,), (2,), (2,),
        (4, 2), (4, 2), (4, 2), (4, 2), (4, 2), (4, 2), (4, 2), (3, 2, 2), (3, 2, 2),
        (4, 2), (4, 2), (4, 2), (4, 2),
        (2, 4), (2, 4), (4, 4), (4, 4), (4,),
    ]
    flops = 2 * 2 * brick * feats * span
    anywhere = pl.BlockSpec(memory_space=pl.ANY)
    scalars = pl.BlockSpec(memory_space=pltpu.SMEM)
    return pl.pallas_call(
        relay_kernel,
        out_shape=(jax.ShapeDtypeStruct((blk, quarter), f32), jax.ShapeDtypeStruct((tok, 4 * feats), bf)),
        in_specs=[anywhere, anywhere, anywhere, anywhere, scalars, scalars],
        out_specs=(anywhere, anywhere),
        scratch_shapes=[
            pltpu.VMEM((brick, span), bf),
            pltpu.VMEM((feats, span), bf),
            pltpu.VMEM((brick, feats), bf),
            pltpu.VMEM((feats, brick), bf),
            pltpu.VMEM((6 * tok, feats), f32),
            pltpu.VMEM((8, 2, blk, cw), bf),
            pltpu.VMEM((2, 4, blk // 2, cw), bf),
            pltpu.VMEM((2, 4, blk, cw), bf),
            pltpu.VMEM((4, blk, cw), f32),
            pltpu.VMEM((rows, feats), bf),
            pltpu.VMEM((rows, feats), bf),
            pltpu.VMEM((rows, feats), bf),
            pltpu.VMEM((blk, quarter), bf),
            pltpu.VMEM((blk, quarter), bf),
        ]
        + [dma(shape) for shape in sems],
        compiler_params=pltpu.CompilerParams(
            collective_id=0, has_side_effects=True, vmem_limit_bytes=63 * 1024 * 1024
        ),
        cost_estimate=pl.CostEstimate(flops=flops, bytes_accessed=32 * 1024 * 1024, transcendentals=0),
        name="relay",
    )(up, saved, weight, noise, levels, plan)


def hand_over(grad, arrived):
    parts = 8
    pieces = []
    for which, one in enumerate((grad, arrived)):
        many = parts if one.shape[0] % (parts * 16) == 0 else 1
        size = one.shape[0] // many
        pieces += [(which, pl.ds(i * size, size)) for i in range(many)]

    def kernel(grad_in, arrived_in, grad_out, arrived_out, grad_held, arrived_held, load_sem, store_sem):
        routes = ((grad_in, grad_held, grad_out), (arrived_in, arrived_held, arrived_out))
        loads, stores = [], []
        for i, (which, place) in enumerate(pieces):
            src, held, dst = (ref.at[place] for ref in routes[which])
            loads.append(pltpu.make_async_copy(src, held, load_sem.at[i]))
            stores.append(pltpu.make_async_copy(held, dst, store_sem.at[i]))
        for one in loads:
            one.start()
        for load, store in zip(loads, stores):
            load.wait()
            store.start()
        for one in stores:
            one.wait()

    anywhere = pl.BlockSpec(memory_space=pl.ANY)
    return pl.pallas_call(
        kernel,
        out_shape=tuple(jax.ShapeDtypeStruct(one.shape, one.dtype) for one in (grad, arrived)),
        in_specs=[anywhere, anywhere],
        out_specs=(anywhere, anywhere),
        scratch_shapes=[pltpu.VMEM(one.shape, one.dtype) for one in (grad, arrived)]
        + [pltpu.SemaphoreType.DMA((len(pieces),)), pltpu.SemaphoreType.DMA((len(pieces),))],
        compiler_params=pltpu.CompilerParams(vmem_limit_bytes=63 * 1024 * 1024),
        name="hand_over",
    )(grad, arrived)


def local(upstream, saved_input, weight, weight_noise, levels, plan):
    tok = upstream.shape[1]
    blk = weight.shape[1]
    saved = saved_input.reshape(saved_input.shape[1], 4, 2, tok, blk)
    grad, arrived = relay_call(upstream[0], saved, weight[0], weight_noise[0], levels[0], plan)
    master, passed = hand_over(grad, arrived)
    return (master[None], passed[None])


def solution(mesh):
    placed = (
        P("pipe", ("dp", "tp"), None),
        P("pipe", None, "dp", "tp"),
        P("pipe", "tp", "dp"),
        P("pipe", "tp", "dp"),
        P("pipe", "tp", "dp"),
        P(),
    )
    return jax.shard_map(
        local,
        mesh=mesh,
        in_specs=placed,
        out_specs=(P("pipe", "tp", "dp"), P("pipe", ("dp", "tp"), None)),
        check_vma=False,
    )
```

```python
import jax
import jax.numpy as jnp
from jax import lax
from jax.experimental import pallas as pl
from jax.experimental.pallas import tpu as pltpu
from jax.sharding import PartitionSpec as P

clip_step = 0.006
MESH = pl.DeviceIdType.MESH
TILE = 128


def aligned(start, size, step=128):
    return pl.ds(pl.multiple_of(start, step), size)


def relay_kernel(
    up, saved, weight_in, noise_in, levels, plan,
    master, passed,
    ubuf, wbuf, cbuf, ctbuf, acc, gbuf, ghalf, gfull, ready, bsend, brecv, bout, weight, noise,
    u_loc, u_sib_s, u_sib_r, u_own_s, u_own_r, u_fwd_s, u_fwd_r,
    c_loc, c_opp_s, c_opp_r, c_sib_s, c_sib_r,
    w_loc, w_own_s, w_own_r, w_leaf_s, w_leaf_r, w_fwd_s, w_fwd_r, w_off_s, w_off_r,
    g_half_s, g_half_r, g_full_s, g_full_r,
    b_sib_s, b_sib_r, b_out_s, b_out_r, m_out,
):
    tok = up.shape[0]
    rows = tok * 4
    near, far = 3 * tok, tok
    quarter = weight.shape[1]
    blk = weight.shape[0]
    half = blk // 2
    subs = 4
    chunks = 2 * subs
    cw = quarter // subs
    tiles = cw // TILE
    feats = 2 * blk
    ahead = 3

    x = lax.axis_index("pipe")
    tp = lax.axis_index("tp")
    dp = lax.axis_index("dp")
    y, zh = tp // 2, tp % 2
    zl, c = dp // 2, dp % 2
    z = 2 * zh + zl
    oc = 1 - c

    def at(xx, yy, zz, cc):
        xx, yy, zz = xx % 4, yy % 4, zz % 4
        return (xx, yy * 2 + zz // 2, (zz % 2) * 2 + cc)

    sib = at(x, y, z, oc)
    opp = at(x, y, z + 2, c)
    ynb = (at(x, y + 1, z, c), at(x, y + 3, z, c))
    znb = (at(x, y, z + 1, c), at(x, y, z + 3, c))
    zp = (zh + zl) % 2
    zside = (zp, 1 - zp)

    barrier = pltpu.get_barrier_semaphore()
    greet = [sib, opp, *ynb, *znb] + [at(x + 1, y + j, z, c) for j in range(4)]
    for one in greet:
        pl.semaphore_signal(barrier, inc=1, device_id=one, device_id_type=MESH)

    @pl.when(x > 0)
    def _():
        pl.semaphore_signal(barrier, inc=1, device_id=at(0, y, z, c), device_id_type=MESH)

    @pl.when(x == 0)
    def _():
        for plane in range(1, 4):
            for step in (1, 3):
                pl.semaphore_signal(barrier, inc=1, device_id=at(plane, y, z + step, c), device_id_type=MESH)

    greeted = len(greet) + 3 - (x + 3) // 4

    def remote(src, dst, s, r, to):
        return pltpu.make_async_remote_copy(
            src_ref=src, dst_ref=dst, send_sem=s, recv_sem=r, device_id=to, device_id_type=MESH
        )

    def each(count, body):
        def one(i, _):
            body(i)
            return 0

        lax.fori_loop(0, count, one, 0)

    def near_rows(cc):
        return aligned(cc * near, near, 16)

    def far_rows(cc):
        return aligned(2 * near + cc * far, far, 16)

    def row(slot, cc):
        return aligned(cc * near + slot * tok, tok, 16)

    def ucol(k):
        return aligned((k % 2) * quarter + (k // 2) * cw, cw)

    def hcol(k, cc):
        return aligned(((zl + k) % 2) * (2 * quarter) + cc * quarter + (k // 2) * cw, cw)

    def u_local(k):
        return pltpu.make_async_copy(up.at[:, hcol(k, c)], ubuf.at[row(0, c), ucol(k)], u_loc.at[k])

    def u_sib(k):
        return remote(up.at[:, hcol(k, oc)], ubuf.at[row(0, c), ucol(k)], u_sib_s.at[k], u_sib_r.at[k], sib)

    def u_own(k, d, mine):
        cc = c if mine else oc
        src = up.at[:, hcol(k, c)] if mine else ubuf.at[row(0, oc), ucol(k)]
        return remote(src, ubuf.at[row(2 - d, cc), ucol(k)], u_own_s.at[k, d, cc], u_own_r.at[k, d, cc], ynb[d])

    def u_own_wait(k, d, cc):
        ref = ubuf.at[row(2 - d, cc), ucol(k)]
        return remote(ref, ref, u_own_s.at[k, d, cc], u_own_r.at[k, d, cc], ynb[d])

    def u_fwd(k, d):
        return remote(
            ubuf.at[row(2 - d, d), ucol(k)], ubuf.at[far_rows(d), ucol(k)], u_fwd_s.at[k, d], u_fwd_r.at[k, d], ynb[d]
        )

    def own_mine(k):
        for d in range(2):
            u_own(k, d, True).start()

    def own_theirs(k):
        u_sib(k).wait_recv()
        for d in range(2):
            u_own(k, d, False).start()

    def pass_on(k):
        for d in range(2):
            u_fwd(k, d).start()

    def w_load(p):
        place = aligned(p * cw, cw)
        return [
            pltpu.make_async_copy(weight_in.at[:, place], weight.at[:, place], w_loc.at[p, 0]),
            pltpu.make_async_copy(noise_in.at[:, place], noise.at[:, place], w_loc.at[p, 1]),
        ]

    def wref(hi, first, count, side, p):
        return wbuf.at[aligned(hi * blk + first, count), aligned(side * quarter + p * cw, cw)]

    def w_own(p, d):
        return remote(
            wref(zh, d * half, half, 0, p), wref(zh, d * half, half, 1, p), w_own_s.at[p, d], w_own_r.at[p, d], znb[d]
        )

    def w_leaf(p, d):
        first = (1 - d) * half
        return remote(
            wref(zh, first, half, 0, p), wref(zh, first, half, 1, p), w_leaf_s.at[p, d], w_leaf_r.at[p, d], znb[d]
        )

    def held(plane, d, u):
        i = ((plane - 1) * 2 + d) * 2 + u
        return wbuf.at[aligned((i // 8) * half, half), aligned((i % 8) * cw, cw)]

    def w_off(d, u):
        to = at(0, y, z + 1 + 2 * d, c)
        return remote(
            wref(zh, (1 - d) * half, half, 0, u + 2), held(x, d, u), w_leaf_s.at[u + 2, d], w_off_r.at[x - 1, d, u], to
        )

    def w_back(plane, d, u):
        dst = wref(zside[1 - d], (1 - d) * half, half, 1, u + 2)
        return remote(
            held(plane, d, u), dst, w_off_s.at[plane - 1, d, u], w_leaf_r.at[u + 2, d], at(plane, y, z, c)
        )

    def w_off_wait(plane, d, u):
        ref = held(plane, d, u)
        return remote(ref, ref, w_off_s.at[plane - 1, d, u], w_off_r.at[plane - 1, d, u], sib)

    def w_fwd(p, d):
        hi = zside[1 - d]
        return remote(
            wref(hi, d * half, half, 1, p), wref(hi, d * half, half, 0, p), w_fwd_s.at[p, d], w_fwd_r.at[p, d], znb[d]
        )

    def w_pass_on(p):
        for d in range(2):
            w_own(p, d).wait_recv()
            w_fwd(p, d).start()

    def clip_weights(p):
        for one in w_load(p):
            one.wait()

        @pl.when(x > 0)
        def _():
            clip_columns(p)

    def clip_columns(p):
        def body(i):
            for j in range(tiles):
                bound = levels[i, p * tiles + j].astype(jnp.float32) * clip_step
                place = (aligned(i * TILE, TILE), aligned(p * cw + j * TILE, TILE))
                noisy = weight[place].astype(jnp.float32) + noise[place].astype(jnp.float32)
                wbuf[aligned(zh * blk + i * TILE, TILE), aligned(p * cw + j * TILE, TILE)] = jnp.minimum(
                    jnp.maximum(noisy, -bound), bound
                ).astype(jnp.bfloat16)

        each(blk // TILE, body)

    def c_load(t):
        slot, other = t // 2, t % 2
        rel = (0, 1, 3, 2)[slot]
        place = (pl.ds(slot * tok, tok), pl.ds(other * blk, blk))
        src = ((y + rel) % 4, (zh + other) % 2)
        return [
            pltpu.make_async_copy(saved.at[(0, *src)], bsend.at[place], c_loc.at[t, 0]),
            pltpu.make_async_copy(saved.at[(1, *src)], bout.at[place], c_loc.at[t, 1]),
        ]

    def ccol(hi):
        return aligned(hi * blk, blk)

    def c_opp(part):
        src = (pl.ds(0, near), pl.ds(near, far))[part]
        dst = (near_rows(c), far_rows(c))[part]
        return remote(
            bout.at[src, pl.ds(blk, blk)], cbuf.at[dst, ccol(zh)], c_opp_s.at[part], c_opp_r.at[part], opp
        )

    def c_sib(part):
        ref = cbuf.at[(near_rows(c), far_rows(c))[part]]
        return remote(ref, ref, c_sib_s.at[part], c_sib_r.at[part], sib)

    def pick_batch():
        for t in range(8):
            for one in c_load(t):
                one.wait()
        second = plan[x].astype(jnp.float32)
        first = 1.0 - second

        def picked(place):
            return (
                bsend[place].astype(jnp.float32) * first + bout[place].astype(jnp.float32) * second
            ).astype(jnp.bfloat16)

        for slot in range(4):
            begin = c * near + slot * tok if slot < 3 else 2 * near + c * far

            def body(i):
                src = aligned(slot * tok + i * 16, 16, 16)
                cbuf[aligned(begin + i * 16, 16, 16), ccol(zh)] = picked((src, pl.ds(0, blk)))
                other = (src, pl.ds(blk, blk))
                bout[other] = picked(other)

            each(tok // 16, body)

    def turn(t):
        place = aligned(t * TILE, TILE)
        ctbuf[:, place] = cbuf[place, :].T

    def grad_chunk(k):
        for d in range(2):
            u_fwd(k, d).wait_recv()

        def body(t):
            b, n = t // 2, t % 2
            hi = (b + zh + (k % 2) * zl) % 2
            cols = aligned((k % 2) * quarter + (k // 2) * cw + n * 256, 256)
            gbuf[k, b, :, aligned(n * 256, 256)] = jnp.dot(
                ctbuf[aligned(hi * blk, blk), :], ubuf[:, cols], preferred_element_type=jnp.float32
            ).astype(jnp.bfloat16)

        each(4, body)

        @pl.when(k % 2 == 0)
        def _():
            for d in range(2):
                g_half(k // 2, d).start()

    def g_half(s, d):
        return remote(
            gbuf.at[2 * s, 1, pl.ds(d * half, half)], ghalf.at[d, s], g_half_s.at[s, d], g_half_r.at[s, d], znb[d]
        )

    def g_full(s, d, h):
        place = pl.ds(h * half, half)
        return remote(
            gbuf.at[2 * s + 1, d, place], gfull.at[d, s, place], g_full_s.at[s, d, h], g_full_r.at[s, d, h], znb[d]
        )

    def combine(s):
        for d in range(2):
            g_half(s, d).wait_recv()
            for i in range(half // 64):
                inner = pl.ds(i * 64, 64)
                place = pl.ds(d * half + i * 64, 64)
                gbuf[2 * s + 1, d, place] = (
                    gbuf[2 * s + 1, d, place].astype(jnp.float32) + ghalf[d, s, inner].astype(jnp.float32)
                ).astype(jnp.bfloat16)
            g_full(s, d, 0).start()
            g_full(s, d, 1).start()

    def master_copy(s):
        return pltpu.make_async_copy(ready.at[s], master.at[:, aligned(s * cw, cw)], m_out.at[s])

    def finish(s):
        for d in range(2):
            for h in range(2):
                g_full(s, d, h).wait_recv()
        scale = 1.0 / (float(rows) * 8.0) ** 0.5

        def body(i):
            line = aligned(i * TILE, TILE)
            for j in range(tiles):
                bound = levels[i, s * tiles + j].astype(jnp.float32) * clip_step
                place = (line, aligned(s * cw + j * TILE, TILE))
                noisy = weight[place].astype(jnp.float32) + noise[place].astype(jnp.float32)
                inner = pl.ds(j * TILE, TILE)
                total = gbuf[2 * s, 0, line, inner].astype(jnp.float32) + gfull[0, s, line, inner].astype(jnp.float32)
                total = total + gfull[1, s, line, inner].astype(jnp.float32)
                ready[s, line, inner] = jnp.where(jnp.abs(noisy) <= bound, total * scale, 0.0)

        each(blk // TILE, body)
        master_copy(s).start()

    def w_ready(p):
        for d in range(2):
            w_leaf(p, d).wait_recv()
            w_fwd(p, d).wait_recv()

    def tile_branch(place, n, sides):
        total = None
        for cols in sides:
            term = lax.dot_general(
                ubuf[place, cols],
                wbuf[aligned(n * 256, 256), cols],
                (((1,), (1,)), ((), ())),
                preferred_element_type=jnp.float32,
            )
            total = term if total is None else total + term
        return total

    def sides_of(s):
        return [aligned(side * quarter + s * cw, cw) for side in range(2)]

    def branch_near(s):
        w_ready(s)

        def body(t):
            place, cols = near_rows(t // 4), aligned((t % 4) * 256, 256)
            acc[place, cols] += tile_branch(place, t % 4, sides_of(s))

        each(2 * (feats // 256), body)

    parts = ((0, tok, (0,)), (tok, 2 * tok, (1, 2)), (near, far, (3,)))

    def b_sib(part, n):
        first, count, _ = parts[part]
        place = (pl.ds(first, count), aligned(n * 256, 256))
        return remote(bsend.at[place], brecv.at[place], b_sib_s.at[part, n], b_sib_r.at[part, n], sib)

    def b_out(n, slot):
        yt = (y + (0, 1, 3, 2)[slot]) % 4
        return remote(
            bout.at[pl.ds(slot * tok, tok), aligned(n * 256, 256)],
            passed.at[:, aligned(y * feats + n * 256, 256)],
            b_out_s.at[n, slot], b_out_r.at[n, slot], at(x + 3, yt, z, c),
        )

    def branch_send(part):
        first, count, slots = parts[part]

        def value(cc, n):
            cols = aligned(n * 256, 256)
            if part == 2:
                return acc[aligned(cc * far, far, 16), cols]
            place = aligned(cc * near + first, count, 16)
            return acc[place, cols] + tile_branch(place, n, sides_of(subs - 1))

        def theirs(n):
            bsend[pl.ds(first, count), aligned(n * 256, 256)] = value(oc, n).astype(jnp.bfloat16)
            b_sib(part, n).start()

        def send(n):
            for slot in slots:
                b_out(n, slot).start()

        def ours(n):
            cols = aligned(n * 256, 256)
            total = value(c, n)
            b_sib(part, n).wait_recv()
            total = total + brecv[pl.ds(first, count), cols].astype(jnp.float32)
            bout[pl.ds(first, count), cols] = total.astype(jnp.bfloat16)
            send(n)

        @pl.when(x > 0)
        def _():
            each(feats // 256, theirs)
            each(feats // 256, ours)

        @pl.when(x == 0)
        def _():
            bout[pl.ds(first, count), :] = jnp.zeros((count, feats), jnp.bfloat16)
            each(feats // 256, send)

    def branch_far():
        whole = pl.ds(2 * near, 2 * far)

        def body(n):
            acc[pl.ds(0, 2 * far), aligned(n * 256, 256)] = tile_branch(
                whole, n, [pl.ds(i * quarter, quarter) for i in range(2)]
            )

        each(feats // 256, body)

    for p in range(subs):
        for one in w_load(p):
            one.start()
    for t in range(8):
        for one in c_load(t):
            one.start()
    clip_weights(0)
    pl.semaphore_wait(barrier, greeted)
    for k in range(2):
        own_mine(k)
        u_sib(k).start()

    @pl.when(x > 0)
    def _():
        for d in range(2):
            w_own(0, d).start()
            w_leaf(0, d).start()

    pick_batch()
    for part in range(2):
        c_opp(part).start()
    for k in range(2):
        own_theirs(k)
    for p in (2, 3):
        clip_weights(p)

    @pl.when(x > 0)
    def _():
        for u in range(2):
            for d in range(2):
                w_off(d, u).start()

    each(chunks - 2, lambda k: u_sib(k + 2).start())
    each(chunks, lambda k: u_local(k).start())
    clip_weights(1)
    acc[...] = jnp.zeros_like(acc)

    def step(k):
        @pl.when(k < chunks)
        def _():
            for d in range(2):
                u_own_wait(k, d, d).wait_recv()

            @pl.when(k >= ahead - 1)
            def _():
                pass_on(k - (ahead - 1))

            @pl.when(k + 2 < chunks)
            def _():
                own_mine(k + 2)
                own_theirs(k + 2)

            @pl.when(k == chunks - 1)
            def _():
                each(ahead - 1, lambda i: pass_on(chunks - ahead + 1 + i))

            u_local(k).wait()
            for d in range(2):
                u_own_wait(k, d, 1 - d).wait_recv()

        @pl.when((x == 0) & ((k == 2) | (k == 4)))
        def _():
            u = (k - 2) // 2
            for plane in (1, 3, 2):
                for d in range(2):
                    w_off_wait(plane, d, u).wait_recv()
                    w_back(plane, d, u).start()

        @pl.when((x > 0) & (k == 1))
        def _():
            w_pass_on(0)

        @pl.when((x > 0) & (k == 2))
        def _():
            for d in range(2):
                w_own(1, d).start()
                w_leaf(1, d).start()
                w_own(2, d).start()

        @pl.when((x > 0) & (k == 3))
        def _():
            for d in range(2):
                w_own(3, d).start()

        @pl.when(k == 3)
        def _():
            for part in range(2):
                c_opp(part).wait_recv()
                c_sib(part).start()
            for part in range(2):
                c_sib(part).wait_recv()
            each((2 * rows) // TILE, turn)

        @pl.when((x > 0) & (k == 4))
        def _():
            w_pass_on(1)
            w_pass_on(2)

        @pl.when((x > 0) & (k == 5))
        def _():
            w_pass_on(3)

        @pl.when(k == 7)
        def _():
            for part in range(2):
                c_opp(part).wait_send()

            @pl.when(x > 0)
            def _():
                w_ready(subs - 1)

            branch_send(0)

        @pl.when((k >= 3) & (k != 7))
        def _():
            grad_chunk(k - 3)

        @pl.when((x > 0) & (k >= 4) & (k < 7))
        def _():
            branch_near(k - 4)

        @pl.when((k == 5) | (k == 7) | (k == 9))
        def _():
            combine((k - 5) // 2)

        @pl.when(k == 7)
        def _():
            branch_send(1)
            grad_chunk(4)

    each(chunks + 3, step)

    @pl.when(x > 0)
    def _():
        branch_far()

    branch_send(2)
    combine(3)

    for part in range(2):
        c_sib(part).wait_send()

    def drain_u(k):
        u_sib(k).wait_send()
        for d in range(2):
            for cc in range(2):
                u_own_wait(k, d, cc).wait_send()
            u_fwd(k, d).wait_send()

    each(chunks, drain_u)

    def drain(s):
        for d in range(2):
            g_half(s, d).wait_send()

        @pl.when(x > 0)
        def _():
            for d in range(2):
                w_own(s, d).wait_send()
                w_leaf(s, d).wait_send()
                w_fwd(s, d).wait_send()
            for part in range(3):
                b_sib(part, s).wait_send()

    each(subs, drain)

    @pl.when(x == 0)
    def _():
        for plane in range(1, 4):
            for d in range(2):
                for u in range(2):
                    w_back(plane, d, u).wait_send()

    each(subs, finish)

    def drain_last(s):
        for d in range(2):
            for h in range(2):
                g_full(s, d, h).wait_send()
        for slot in range(4):
            b_out(s, slot).wait()
        master_copy(s).wait()

    each(subs, drain_last)


def relay_call(up, saved, weight, noise, levels, plan):
    tok, width = up.shape
    blk, quarter = weight.shape
    rows = 4 * tok
    brick, feats = 2 * rows, 2 * blk
    span = 2 * quarter
    cw = quarter // 4
    bf, f32 = jnp.bfloat16, jnp.float32
    dma = pltpu.SemaphoreType.DMA
    sems = [
        (8,), (8,), (8,), (8, 2, 2), (8, 2, 2), (8, 2), (8, 2),
        (8, 2), (2,), (2,), (2,), (2,),
        (4, 2), (4, 2), (4, 2), (4, 2), (4, 2), (4, 2), (4, 2), (3, 2, 2), (3, 2, 2),
        (4, 2), (4, 2), (4, 2, 2), (4, 2, 2),
        (3, 4), (3, 4), (4, 4), (4, 4), (4,),
    ]
    flops = 2 * 2 * brick * feats * span
    anywhere = pl.BlockSpec(memory_space=pl.ANY)
    scalars = pl.BlockSpec(memory_space=pltpu.SMEM)
    return pl.pallas_call(
        relay_kernel,
        out_shape=(jax.ShapeDtypeStruct((blk, quarter), f32), jax.ShapeDtypeStruct((tok, 4 * feats), bf)),
        in_specs=[anywhere, anywhere, anywhere, anywhere, scalars, scalars],
        out_specs=(anywhere, anywhere),
        scratch_shapes=[
            pltpu.VMEM((brick, span), bf),
            pltpu.VMEM((feats, span), bf),
            pltpu.VMEM((brick, feats), bf),
            pltpu.VMEM((feats, brick), bf),
            pltpu.VMEM((6 * tok, feats), f32),
            pltpu.VMEM((8, 2, blk, cw), bf),
            pltpu.VMEM((2, 4, blk // 2, cw), bf),
            pltpu.VMEM((2, 4, blk, cw), bf),
            pltpu.VMEM((4, blk, cw), f32),
            pltpu.VMEM((rows, feats), bf),
            pltpu.VMEM((rows, feats), bf),
            pltpu.VMEM((rows, feats), bf),
            pltpu.VMEM((blk, quarter), bf),
            pltpu.VMEM((blk, quarter), bf),
        ]
        + [dma(shape) for shape in sems],
        compiler_params=pltpu.CompilerParams(
            collective_id=0, has_side_effects=True, vmem_limit_bytes=63 * 1024 * 1024
        ),
        cost_estimate=pl.CostEstimate(flops=flops, bytes_accessed=32 * 1024 * 1024, transcendentals=0),
        name="relay",
    )(up, saved, weight, noise, levels, plan)


def hand_over(grad, arrived):
    pieces = []
    for which, one in enumerate((grad, arrived)):
        size = -(-one.shape[0] // (64, 32)[which]) * 16
        pieces += [
            (which, pl.ds(begin, min(size, one.shape[0] - begin))) for begin in range(0, one.shape[0], size)
        ]

    def kernel(grad_in, arrived_in, grad_out, arrived_out, grad_held, arrived_held, load_sem, store_sem):
        routes = ((grad_in, grad_held, grad_out), (arrived_in, arrived_held, arrived_out))
        loads, stores = [], []
        for i, (which, place) in enumerate(pieces):
            src, held, dst = (ref.at[place] for ref in routes[which])
            loads.append(pltpu.make_async_copy(src, held, load_sem.at[i]))
            stores.append(pltpu.make_async_copy(held, dst, store_sem.at[i]))
        for one in loads:
            one.start()
        for load, store in zip(loads, stores):
            load.wait()
            store.start()
        for one in stores:
            one.wait()

    anywhere = pl.BlockSpec(memory_space=pl.ANY)
    return pl.pallas_call(
        kernel,
        out_shape=tuple(jax.ShapeDtypeStruct(one.shape, one.dtype) for one in (grad, arrived)),
        in_specs=[anywhere, anywhere],
        out_specs=(anywhere, anywhere),
        scratch_shapes=[pltpu.VMEM(one.shape, one.dtype) for one in (grad, arrived)]
        + [pltpu.SemaphoreType.DMA((len(pieces),)), pltpu.SemaphoreType.DMA((len(pieces),))],
        compiler_params=pltpu.CompilerParams(vmem_limit_bytes=63 * 1024 * 1024),
        name="hand_over",
    )(grad, arrived)


def local(upstream, saved_input, weight, weight_noise, levels, plan):
    tok = upstream.shape[1]
    blk = weight.shape[1]
    saved = saved_input.reshape(saved_input.shape[1], 4, 2, tok, blk)
    grad, arrived = relay_call(upstream[0], saved, weight[0], weight_noise[0], levels[0], plan)
    master, passed = hand_over(grad, arrived)
    return (master[None], passed[None])


def solution(mesh):
    placed = (
        P("pipe", ("dp", "tp"), None),
        P("pipe", None, "dp", "tp"),
        P("pipe", "tp", "dp"),
        P("pipe", "tp", "dp"),
        P("pipe", "tp", "dp"),
        P(),
    )
    return jax.shard_map(
        local,
        mesh=mesh,
        in_specs=placed,
        out_specs=(P("pipe", "tp", "dp"), P("pipe", ("dp", "tp"), None)),
        check_vma=False,
    )
```

```python
import jax
import jax.numpy as jnp
from jax import lax
from jax.experimental import pallas as pl
from jax.experimental.pallas import tpu as pltpu
from jax.sharding import PartitionSpec as P

clip_step = 0.006
MESH = pl.DeviceIdType.MESH
TILE = 128


def aligned(start, size, step=128):
    return pl.ds(pl.multiple_of(start, step), size)


def relay_kernel(
    up, saved, weight_in, noise_in, levels, plan,
    master, passed,
    ubuf, wbuf, cbuf, ctbuf, acc, gbuf, ghalf, gfull, ready, bsend, brecv, bout, weight, noise,
    u_loc, u_sib_s, u_sib_r, u_own_s, u_own_r, u_fwd_s, u_fwd_r,
    c_loc, c_opp_s, c_opp_r, c_sib_s, c_sib_r,
    w_loc, w_own_s, w_own_r, w_leaf_s, w_leaf_r, w_fwd_s, w_fwd_r, w_off_s, w_off_r,
    g_half_s, g_half_r, g_full_s, g_full_r,
    b_sib_s, b_sib_r, b_out_s, b_out_r, m_out,
):
    tok = up.shape[0]
    rows = tok * 4
    near, far = 3 * tok, tok
    quarter = weight.shape[1]
    blk = weight.shape[0]
    half = blk // 2
    subs = 4
    chunks = 2 * subs
    cw = quarter // subs
    tiles = cw // TILE
    feats = 2 * blk
    ahead = 3

    x = lax.axis_index("pipe")
    tp = lax.axis_index("tp")
    dp = lax.axis_index("dp")
    y, zh = tp // 2, tp % 2
    zl, c = dp // 2, dp % 2
    z = 2 * zh + zl
    oc = 1 - c

    def at(xx, yy, zz, cc):
        xx, yy, zz = xx % 4, yy % 4, zz % 4
        return (xx, yy * 2 + zz // 2, (zz % 2) * 2 + cc)

    sib = at(x, y, z, oc)
    opp = at(x, y, z + 2, c)
    ynb = (at(x, y + 1, z, c), at(x, y + 3, z, c))
    znb = (at(x, y, z + 1, c), at(x, y, z + 3, c))
    zp = (zh + zl) % 2
    zside = (zp, 1 - zp)

    for place in (pl.ds(0, cw),):
        pltpu.make_async_copy(weight_in.at[:, place], weight.at[:, place], w_loc.at[0, 0]).start()
        pltpu.make_async_copy(noise_in.at[:, place], noise.at[:, place], w_loc.at[0, 1]).start()

    barrier = pltpu.get_barrier_semaphore()
    greet = [sib, opp, *ynb, *znb] + [at(x + 1, y + j, z, c) for j in range(4)]
    for one in greet:
        pl.semaphore_signal(barrier, inc=1, device_id=one, device_id_type=MESH)

    @pl.when(x > 0)
    def _():
        pl.semaphore_signal(barrier, inc=1, device_id=at(0, y, z, c), device_id_type=MESH)

    @pl.when(x == 0)
    def _():
        for plane in range(1, 4):
            for step in (1, 3):
                pl.semaphore_signal(barrier, inc=1, device_id=at(plane, y, z + step, c), device_id_type=MESH)

    greeted = len(greet) + 3 - (x + 3) // 4

    def remote(src, dst, s, r, to):
        return pltpu.make_async_remote_copy(
            src_ref=src, dst_ref=dst, send_sem=s, recv_sem=r, device_id=to, device_id_type=MESH
        )

    def each(count, body):
        def one(i, _):
            body(i)
            return 0

        lax.fori_loop(0, count, one, 0)

    def near_rows(cc):
        return aligned(cc * near, near, 16)

    def far_rows(cc):
        return aligned(2 * near + cc * far, far, 16)

    def row(slot, cc):
        return aligned(cc * near + slot * tok, tok, 16)

    def ucol(k):
        return aligned((k % 2) * quarter + (k // 2) * cw, cw)

    def hcol(k, cc):
        return aligned(((zl + k) % 2) * (2 * quarter) + cc * quarter + (k // 2) * cw, cw)

    def u_local(k):
        return pltpu.make_async_copy(up.at[:, hcol(k, c)], ubuf.at[row(0, c), ucol(k)], u_loc.at[k])

    def u_sib(k):
        return remote(up.at[:, hcol(k, oc)], ubuf.at[row(0, c), ucol(k)], u_sib_s.at[k], u_sib_r.at[k], sib)

    def u_own(k, d, mine):
        cc = c if mine else oc
        src = up.at[:, hcol(k, c)] if mine else ubuf.at[row(0, oc), ucol(k)]
        return remote(src, ubuf.at[row(2 - d, cc), ucol(k)], u_own_s.at[k, d, cc], u_own_r.at[k, d, cc], ynb[d])

    def u_own_wait(k, d, cc):
        ref = ubuf.at[row(2 - d, cc), ucol(k)]
        return remote(ref, ref, u_own_s.at[k, d, cc], u_own_r.at[k, d, cc], ynb[d])

    def u_fwd(k, d):
        return remote(
            ubuf.at[row(2 - d, d), ucol(k)], ubuf.at[far_rows(d), ucol(k)], u_fwd_s.at[k, d], u_fwd_r.at[k, d], ynb[d]
        )

    def own_mine(k):
        for d in range(2):
            u_own(k, d, True).start()

    def own_theirs(k):
        u_sib(k).wait_recv()
        for d in range(2):
            u_own(k, d, False).start()

    def pass_on(k):
        for d in range(2):
            u_fwd(k, d).start()

    def w_load(p):
        place = aligned(p * cw, cw)
        return [
            pltpu.make_async_copy(weight_in.at[:, place], weight.at[:, place], w_loc.at[p, 0]),
            pltpu.make_async_copy(noise_in.at[:, place], noise.at[:, place], w_loc.at[p, 1]),
        ]

    def wref(hi, first, count, side, p):
        return wbuf.at[aligned(hi * blk + first, count), aligned(side * quarter + p * cw, cw)]

    def w_own(p, d):
        return remote(
            wref(zh, d * half, half, 0, p), wref(zh, d * half, half, 1, p), w_own_s.at[p, d], w_own_r.at[p, d], znb[d]
        )

    def w_leaf(p, d):
        first = (1 - d) * half
        return remote(
            wref(zh, first, half, 0, p), wref(zh, first, half, 1, p), w_leaf_s.at[p, d], w_leaf_r.at[p, d], znb[d]
        )

    def held(plane, d, u):
        i = ((plane - 1) * 2 + d) * 2 + u
        return wbuf.at[aligned((i // 8) * half, half), aligned((i % 8) * cw, cw)]

    def w_off(d, u):
        to = at(0, y, z + 1 + 2 * d, c)
        return remote(
            wref(zh, (1 - d) * half, half, 0, u + 2), held(x, d, u), w_leaf_s.at[u + 2, d], w_off_r.at[x - 1, d, u], to
        )

    def w_back(plane, d, u):
        dst = wref(zside[1 - d], (1 - d) * half, half, 1, u + 2)
        return remote(
            held(plane, d, u), dst, w_off_s.at[plane - 1, d, u], w_leaf_r.at[u + 2, d], at(plane, y, z, c)
        )

    def w_off_wait(plane, d, u):
        ref = held(plane, d, u)
        return remote(ref, ref, w_off_s.at[plane - 1, d, u], w_off_r.at[plane - 1, d, u], sib)

    def w_fwd(p, d):
        hi = zside[1 - d]
        return remote(
            wref(hi, d * half, half, 1, p), wref(hi, d * half, half, 0, p), w_fwd_s.at[p, d], w_fwd_r.at[p, d], znb[d]
        )

    def w_pass_on(p):
        for d in range(2):
            w_own(p, d).wait_recv()
            w_fwd(p, d).start()

    def clip_weights(p):
        for one in w_load(p):
            one.wait()

        @pl.when(x > 0)
        def _():
            clip_columns(p)

    def clip_columns(p):
        def body(i):
            for j in range(tiles):
                bound = levels[i, p * tiles + j].astype(jnp.float32) * clip_step
                place = (aligned(i * TILE, TILE), aligned(p * cw + j * TILE, TILE))
                noisy = weight[place].astype(jnp.float32) + noise[place].astype(jnp.float32)
                wbuf[aligned(zh * blk + i * TILE, TILE), aligned(p * cw + j * TILE, TILE)] = jnp.minimum(
                    jnp.maximum(noisy, -bound), bound
                ).astype(jnp.bfloat16)

        each(blk // TILE, body)

    def c_load(t):
        slot, other = t // 2, t % 2
        rel = (0, 1, 3, 2)[slot]
        place = (pl.ds(slot * tok, tok), pl.ds(other * blk, blk))
        src = ((y + rel) % 4, (zh + other) % 2)
        return [
            pltpu.make_async_copy(saved.at[(0, *src)], bsend.at[place], c_loc.at[t, 0]),
            pltpu.make_async_copy(saved.at[(1, *src)], bout.at[place], c_loc.at[t, 1]),
        ]

    def ccol(hi):
        return aligned(hi * blk, blk)

    def c_opp(part):
        src = (pl.ds(0, near), pl.ds(near, far))[part]
        dst = (near_rows(c), far_rows(c))[part]
        return remote(
            bout.at[src, pl.ds(blk, blk)], cbuf.at[dst, ccol(zh)], c_opp_s.at[part], c_opp_r.at[part], opp
        )

    def c_sib(part):
        ref = cbuf.at[(near_rows(c), far_rows(c))[part]]
        return remote(ref, ref, c_sib_s.at[part], c_sib_r.at[part], sib)

    def pick_batch():
        for t in range(8):
            for one in c_load(t):
                one.wait()
        second = plan[x].astype(jnp.float32)
        first = 1.0 - second

        def picked(place):
            return (
                bsend[place].astype(jnp.float32) * first + bout[place].astype(jnp.float32) * second
            ).astype(jnp.bfloat16)

        for slot in range(4):
            begin = c * near + slot * tok if slot < 3 else 2 * near + c * far

            def body(i):
                src = aligned(slot * tok + i * 16, 16, 16)
                cbuf[aligned(begin + i * 16, 16, 16), ccol(zh)] = picked((src, pl.ds(0, blk)))
                other = (src, pl.ds(blk, blk))
                bout[other] = picked(other)

            each(tok // 16, body)

    def turn(t):
        place = aligned(t * TILE, TILE)
        ctbuf[:, place] = cbuf[place, :].T

    def grad_chunk(k):
        for d in range(2):
            u_fwd(k, d).wait_recv()

        def body(t):
            b, n = t // 2, t % 2
            hi = (b + zh + (k % 2) * zl) % 2
            cols = aligned((k % 2) * quarter + (k // 2) * cw + n * 256, 256)
            gbuf[k, b, :, aligned(n * 256, 256)] = jnp.dot(
                ctbuf[aligned(hi * blk, blk), :], ubuf[:, cols], preferred_element_type=jnp.float32
            ).astype(jnp.bfloat16)

        each(4, body)

        @pl.when(k % 2 == 0)
        def _():
            for d in range(2):
                g_half(k // 2, d).start()

    def g_half(s, d):
        return remote(
            gbuf.at[2 * s, 1, pl.ds(d * half, half)], ghalf.at[d, s], g_half_s.at[s, d], g_half_r.at[s, d], znb[d]
        )

    def g_full(s, d):
        return remote(gbuf.at[2 * s + 1, d], gfull.at[d, s], g_full_s.at[s, d], g_full_r.at[s, d], znb[d])

    def combine(s):
        for d in range(2):
            g_half(s, d).wait_recv()
            for i in range(half // 64):
                inner = pl.ds(i * 64, 64)
                place = pl.ds(d * half + i * 64, 64)
                gbuf[2 * s + 1, d, place] = (
                    gbuf[2 * s + 1, d, place].astype(jnp.float32) + ghalf[d, s, inner].astype(jnp.float32)
                ).astype(jnp.bfloat16)
            g_full(s, d).start()

    def master_copy(s):
        return pltpu.make_async_copy(ready.at[s], master.at[:, aligned(s * cw, cw)], m_out.at[s])

    def finish(s):
        for d in range(2):
            g_full(s, d).wait_recv()
        scale = 1.0 / (float(rows) * 8.0) ** 0.5

        def body(i):
            line = aligned(i * TILE, TILE)
            for j in range(tiles):
                bound = levels[i, s * tiles + j].astype(jnp.float32) * clip_step
                place = (line, aligned(s * cw + j * TILE, TILE))
                noisy = weight[place].astype(jnp.float32) + noise[place].astype(jnp.float32)
                inner = pl.ds(j * TILE, TILE)
                total = gbuf[2 * s, 0, line, inner].astype(jnp.float32) + gfull[0, s, line, inner].astype(jnp.float32)
                total = total + gfull[1, s, line, inner].astype(jnp.float32)
                ready[s, line, inner] = jnp.where(jnp.abs(noisy) <= bound, total * scale, 0.0)

        each(blk // TILE, body)
        master_copy(s).start()

    def w_ready(p):
        for d in range(2):
            w_leaf(p, d).wait_recv()
            w_fwd(p, d).wait_recv()

    def tile_branch(place, n, sides):
        total = None
        for cols in sides:
            term = lax.dot_general(
                ubuf[place, cols],
                wbuf[aligned(n * 256, 256), cols],
                (((1,), (1,)), ((), ())),
                preferred_element_type=jnp.float32,
            )
            total = term if total is None else total + term
        return total

    def sides_of(s):
        return [aligned(side * quarter + s * cw, cw) for side in range(2)]

    def branch_near(s):
        w_ready(s)

        def body(t):
            place, cols = near_rows(t // 4), aligned((t % 4) * 256, 256)
            acc[place, cols] += tile_branch(place, t % 4, sides_of(s))

        each(2 * (feats // 256), body)

    parts = ((0, tok, (0,)), (tok, 2 * tok, (1, 2)), (near, far, (3,)))

    def b_sib(part, n):
        first, count, _ = parts[part]
        place = (pl.ds(first, count), aligned(n * 256, 256))
        return remote(bsend.at[place], brecv.at[place], b_sib_s.at[part, n], b_sib_r.at[part, n], sib)

    def b_out(n, slot):
        yt = (y + (0, 1, 3, 2)[slot]) % 4
        return remote(
            bout.at[pl.ds(slot * tok, tok), aligned(n * 256, 256)],
            passed.at[:, aligned(y * feats + n * 256, 256)],
            b_out_s.at[n, slot], b_out_r.at[n, slot], at(x + 3, yt, z, c),
        )

    def branch_send(part):
        first, count, slots = parts[part]

        def value(cc, n):
            cols = aligned(n * 256, 256)
            if part == 2:
                return acc[aligned(cc * far, far, 16), cols]
            place = aligned(cc * near + first, count, 16)
            return acc[place, cols] + tile_branch(place, n, sides_of(subs - 1))

        def theirs(n):
            bsend[pl.ds(first, count), aligned(n * 256, 256)] = value(oc, n).astype(jnp.bfloat16)
            b_sib(part, n).start()

        def send(n):
            for slot in slots:
                b_out(n, slot).start()

        def ours(n):
            cols = aligned(n * 256, 256)
            total = value(c, n)
            b_sib(part, n).wait_recv()
            total = total + brecv[pl.ds(first, count), cols].astype(jnp.float32)
            bout[pl.ds(first, count), cols] = total.astype(jnp.bfloat16)
            send(n)

        @pl.when(x > 0)
        def _():
            each(feats // 256, theirs)
            each(feats // 256, ours)

        @pl.when(x == 0)
        def _():
            bout[pl.ds(first, count), :] = jnp.zeros((count, feats), jnp.bfloat16)
            each(feats // 256, send)

    def branch_far():
        whole = pl.ds(2 * near, 2 * far)

        def body(n):
            acc[pl.ds(0, 2 * far), aligned(n * 256, 256)] = tile_branch(
                whole, n, [pl.ds(i * quarter, quarter) for i in range(2)]
            )

        each(feats // 256, body)

    for t in range(8):
        for one in c_load(t):
            one.start()
    clip_weights(0)
    for p in range(1, subs):
        for one in w_load(p):
            one.start()
    pl.semaphore_wait(barrier, greeted)
    for k in range(2):
        own_mine(k)
        u_sib(k).start()

    @pl.when(x > 0)
    def _():
        for d in range(2):
            w_own(0, d).start()
            w_leaf(0, d).start()

    pick_batch()
    for part in range(2):
        c_opp(part).start()
    for k in range(2):
        own_theirs(k)
    for p in (2, 3):
        clip_weights(p)

    @pl.when(x > 0)
    def _():
        for u in range(2):
            for d in range(2):
                w_off(d, u).start()

    each(chunks - 2, lambda k: u_sib(k + 2).start())
    each(chunks, lambda k: u_local(k).start())
    clip_weights(1)
    acc[...] = jnp.zeros_like(acc)

    def step(k):
        @pl.when(k < chunks)
        def _():
            for d in range(2):
                u_own_wait(k, d, d).wait_recv()

            @pl.when(k >= ahead - 1)
            def _():
                pass_on(k - (ahead - 1))

            @pl.when(k + 2 < chunks)
            def _():
                own_mine(k + 2)
                own_theirs(k + 2)

            @pl.when(k == chunks - 1)
            def _():
                each(ahead - 1, lambda i: pass_on(chunks - ahead + 1 + i))

            u_local(k).wait()
            for d in range(2):
                u_own_wait(k, d, 1 - d).wait_recv()

        @pl.when((x == 0) & ((k == 2) | (k == 4)))
        def _():
            u = (k - 2) // 2
            for plane in (1, 3, 2):
                for d in range(2):
                    w_off_wait(plane, d, u).wait_recv()
                    w_back(plane, d, u).start()

        @pl.when((x > 0) & (k == 1))
        def _():
            w_pass_on(0)

        @pl.when((x > 0) & (k == 2))
        def _():
            for d in range(2):
                w_own(1, d).start()
                w_leaf(1, d).start()
                w_own(2, d).start()

        @pl.when((x > 0) & (k == 3))
        def _():
            for d in range(2):
                w_own(3, d).start()

        @pl.when(k == 3)
        def _():
            for part in range(2):
                c_opp(part).wait_recv()
                c_sib(part).start()
            for part in range(2):
                c_sib(part).wait_recv()
            each((2 * rows) // TILE, turn)

        @pl.when((x > 0) & (k == 4))
        def _():
            w_pass_on(1)
            w_pass_on(2)

        @pl.when((x > 0) & (k == 5))
        def _():
            w_pass_on(3)

        @pl.when(k == 7)
        def _():
            for part in range(2):
                c_opp(part).wait_send()

            @pl.when(x > 0)
            def _():
                w_ready(subs - 1)

            branch_send(0)

        @pl.when((k >= 3) & (k != 7))
        def _():
            grad_chunk(k - 3)

        @pl.when((x > 0) & (k >= 4) & (k < 7))
        def _():
            branch_near(k - 4)

        @pl.when((k == 5) | (k == 7) | (k == 9))
        def _():
            combine((k - 5) // 2)

        @pl.when(k == 7)
        def _():
            branch_send(1)
            grad_chunk(4)

    each(chunks + 3, step)

    @pl.when(x > 0)
    def _():
        branch_far()

    branch_send(2)
    combine(3)

    for part in range(2):
        c_sib(part).wait_send()

    def drain_u(k):
        u_sib(k).wait_send()
        for d in range(2):
            for cc in range(2):
                u_own_wait(k, d, cc).wait_send()
            u_fwd(k, d).wait_send()

    each(chunks, drain_u)

    def drain(s):
        for d in range(2):
            g_half(s, d).wait_send()

        @pl.when(x > 0)
        def _():
            for d in range(2):
                w_own(s, d).wait_send()
                w_leaf(s, d).wait_send()
                w_fwd(s, d).wait_send()
            for part in range(3):
                b_sib(part, s).wait_send()

    each(subs, drain)

    @pl.when(x == 0)
    def _():
        for plane in range(1, 4):
            for d in range(2):
                for u in range(2):
                    w_back(plane, d, u).wait_send()

    each(subs - 1, finish)

    def drain_last(s):
        for slot in range(4):
            b_out(s, slot).wait()

    each(subs, drain_last)
    for s in range(subs - 1):
        master_copy(s).wait()
    finish(subs - 1)
    for s in range(subs):
        for d in range(2):
            g_full(s, d).wait_send()
    master_copy(subs - 1).wait()


def relay_call(up, saved, weight, noise, levels, plan):
    tok, width = up.shape
    blk, quarter = weight.shape
    rows = 4 * tok
    brick, feats = 2 * rows, 2 * blk
    span = 2 * quarter
    cw = quarter // 4
    bf, f32 = jnp.bfloat16, jnp.float32
    dma = pltpu.SemaphoreType.DMA
    sems = [
        (8,), (8,), (8,), (8, 2, 2), (8, 2, 2), (8, 2), (8, 2),
        (8, 2), (2,), (2,), (2,), (2,),
        (4, 2), (4, 2), (4, 2), (4, 2), (4, 2), (4, 2), (4, 2), (3, 2, 2), (3, 2, 2),
        (4, 2), (4, 2), (4, 2), (4, 2),
        (3, 4), (3, 4), (4, 4), (4, 4), (4,),
    ]
    flops = 2 * 2 * brick * feats * span
    anywhere = pl.BlockSpec(memory_space=pl.ANY)
    scalars = pl.BlockSpec(memory_space=pltpu.SMEM)
    return pl.pallas_call(
        relay_kernel,
        out_shape=(jax.ShapeDtypeStruct((blk, quarter), f32), jax.ShapeDtypeStruct((tok, 4 * feats), bf)),
        in_specs=[anywhere, anywhere, anywhere, anywhere, scalars, scalars],
        out_specs=(anywhere, anywhere),
        scratch_shapes=[
            pltpu.VMEM((brick, span), bf),
            pltpu.VMEM((feats, span), bf),
            pltpu.VMEM((brick, feats), bf),
            pltpu.VMEM((feats, brick), bf),
            pltpu.VMEM((6 * tok, feats), f32),
            pltpu.VMEM((8, 2, blk, cw), bf),
            pltpu.VMEM((2, 4, blk // 2, cw), bf),
            pltpu.VMEM((2, 4, blk, cw), bf),
            pltpu.VMEM((4, blk, cw), f32),
            pltpu.VMEM((rows, feats), bf),
            pltpu.VMEM((rows, feats), bf),
            pltpu.VMEM((rows, feats), bf),
            pltpu.VMEM((blk, quarter), bf),
            pltpu.VMEM((blk, quarter), bf),
        ]
        + [dma(shape) for shape in sems],
        compiler_params=pltpu.CompilerParams(
            collective_id=0, has_side_effects=True, vmem_limit_bytes=63 * 1024 * 1024
        ),
        cost_estimate=pl.CostEstimate(flops=flops, bytes_accessed=32 * 1024 * 1024, transcendentals=0),
        name="relay",
    )(up, saved, weight, noise, levels, plan)


def hand_over(grad, arrived):
    pieces = []
    for which, one in enumerate((grad, arrived)):
        size = -(-one.shape[0] // (32, 32)[which]) * 16
        pieces += [
            (which, pl.ds(begin, min(size, one.shape[0] - begin))) for begin in range(0, one.shape[0], size)
        ]

    def kernel(grad_in, arrived_in, grad_out, arrived_out, grad_held, arrived_held, load_sem, store_sem):
        routes = ((grad_in, grad_held, grad_out), (arrived_in, arrived_held, arrived_out))
        loads, stores = [], []
        for i, (which, place) in enumerate(pieces):
            src, held, dst = (ref.at[place] for ref in routes[which])
            loads.append(pltpu.make_async_copy(src, held, load_sem.at[i]))
            stores.append(pltpu.make_async_copy(held, dst, store_sem.at[i]))
        for one in loads:
            one.start()
        for load, store in zip(loads, stores):
            load.wait()
            store.start()
        for one in stores:
            one.wait()

    anywhere = pl.BlockSpec(memory_space=pl.ANY)
    return pl.pallas_call(
        kernel,
        out_shape=tuple(jax.ShapeDtypeStruct(one.shape, one.dtype) for one in (grad, arrived)),
        in_specs=[anywhere, anywhere],
        out_specs=(anywhere, anywhere),
        scratch_shapes=[pltpu.VMEM(one.shape, one.dtype) for one in (grad, arrived)]
        + [pltpu.SemaphoreType.DMA((len(pieces),)), pltpu.SemaphoreType.DMA((len(pieces),))],
        compiler_params=pltpu.CompilerParams(vmem_limit_bytes=63 * 1024 * 1024),
        name="hand_over",
    )(grad, arrived)


def local(upstream, saved_input, weight, weight_noise, levels, plan):
    tok = upstream.shape[1]
    blk = weight.shape[1]
    saved = saved_input.reshape(saved_input.shape[1], 4, 2, tok, blk)
    grad, arrived = relay_call(upstream[0], saved, weight[0], weight_noise[0], levels[0], plan)
    master, passed = hand_over(grad, arrived)
    return (master[None], passed[None])


def solution(mesh):
    placed = (
        P("pipe", ("dp", "tp"), None),
        P("pipe", None, "dp", "tp"),
        P("pipe", "tp", "dp"),
        P("pipe", "tp", "dp"),
        P("pipe", "tp", "dp"),
        P(),
    )
    return jax.shard_map(
        local,
        mesh=mesh,
        in_specs=placed,
        out_specs=(P("pipe", "tp", "dp"), P("pipe", ("dp", "tp"), None)),
        check_vma=False,
    )
```

```python
import jax
import jax.numpy as jnp
from jax import lax
from jax.experimental import pallas as pl
from jax.experimental.pallas import tpu as pltpu
from jax.sharding import PartitionSpec as P

clip_step = 0.006
MESH = pl.DeviceIdType.MESH
TILE = 128


def aligned(start, size, step=128):
    return pl.ds(pl.multiple_of(start, step), size)


def relay_kernel(
    up, saved, weight_in, noise_in, levels, plan,
    master, passed,
    ubuf, wbuf, cbuf, ctbuf, acc, gbuf, ghalf, gfull, ready, bsend, brecv, bout, weight, noise,
    u_loc, u_sib_s, u_sib_r, u_own_s, u_own_r, u_fwd_s, u_fwd_r,
    c_loc, c_opp_s, c_opp_r, c_sib_s, c_sib_r,
    w_loc, w_own_s, w_own_r, w_leaf_s, w_leaf_r, w_fwd_s, w_fwd_r, w_off_s, w_off_r,
    g_half_s, g_half_r, g_full_s, g_full_r,
    b_sib_s, b_sib_r, b_out_s, b_out_r, m_out,
):
    tok = up.shape[0]
    rows = tok * 4
    near, far = 3 * tok, tok
    quarter = weight.shape[1]
    blk = weight.shape[0]
    half = blk // 2
    subs = 4
    chunks = 2 * subs
    cw = quarter // subs
    tiles = cw // TILE
    feats = 2 * blk
    ahead = 3

    x = lax.axis_index("pipe")
    tp = lax.axis_index("tp")
    dp = lax.axis_index("dp")
    y, zh = tp // 2, tp % 2
    zl, c = dp // 2, dp % 2
    z = 2 * zh + zl
    oc = 1 - c

    def at(xx, yy, zz, cc):
        xx, yy, zz = xx % 4, yy % 4, zz % 4
        return (xx, yy * 2 + zz // 2, (zz % 2) * 2 + cc)

    sib = at(x, y, z, oc)
    opp = at(x, y, z + 2, c)
    ynb = (at(x, y + 1, z, c), at(x, y + 3, z, c))
    znb = (at(x, y, z + 1, c), at(x, y, z + 3, c))
    zp = (zh + zl) % 2
    zside = (zp, 1 - zp)

    for place in (pl.ds(0, cw),):
        pltpu.make_async_copy(weight_in.at[:, place], weight.at[:, place], w_loc.at[0, 0]).start()
        pltpu.make_async_copy(noise_in.at[:, place], noise.at[:, place], w_loc.at[0, 1]).start()

    barrier = pltpu.get_barrier_semaphore()
    greet = [sib, opp, *ynb, *znb] + [at(x + 1, y + j, z, c) for j in range(4)]
    for one in greet:
        pl.semaphore_signal(barrier, inc=1, device_id=one, device_id_type=MESH)

    @pl.when(x > 0)
    def _():
        pl.semaphore_signal(barrier, inc=1, device_id=at(0, y, z, c), device_id_type=MESH)

    @pl.when(x == 0)
    def _():
        for plane in range(1, 4):
            for step in (1, 3):
                pl.semaphore_signal(barrier, inc=1, device_id=at(plane, y, z + step, c), device_id_type=MESH)

    greeted = len(greet) + 3 - (x + 3) // 4

    def remote(src, dst, s, r, to):
        return pltpu.make_async_remote_copy(
            src_ref=src, dst_ref=dst, send_sem=s, recv_sem=r, device_id=to, device_id_type=MESH
        )

    def each(count, body):
        def one(i, _):
            body(i)
            return 0

        lax.fori_loop(0, count, one, 0)

    def near_rows(cc):
        return aligned(cc * near, near, 16)

    def far_rows(cc):
        return aligned(2 * near + cc * far, far, 16)

    def row(slot, cc):
        return aligned(cc * near + slot * tok, tok, 16)

    def ucol(k):
        return aligned((k % 2) * quarter + (k // 2) * cw, cw)

    def hcol(k, cc):
        return aligned(((zl + k) % 2) * (2 * quarter) + cc * quarter + (k // 2) * cw, cw)

    def u_local(k):
        return pltpu.make_async_copy(up.at[:, hcol(k, c)], ubuf.at[row(0, c), ucol(k)], u_loc.at[k])

    def u_sib(k):
        return remote(up.at[:, hcol(k, oc)], ubuf.at[row(0, c), ucol(k)], u_sib_s.at[k], u_sib_r.at[k], sib)

    def u_own(k, d, mine):
        cc = c if mine else oc
        src = up.at[:, hcol(k, c)] if mine else ubuf.at[row(0, oc), ucol(k)]
        return remote(src, ubuf.at[row(2 - d, cc), ucol(k)], u_own_s.at[k, d, cc], u_own_r.at[k, d, cc], ynb[d])

    def u_own_wait(k, d, cc):
        ref = ubuf.at[row(2 - d, cc), ucol(k)]
        return remote(ref, ref, u_own_s.at[k, d, cc], u_own_r.at[k, d, cc], ynb[d])

    def u_fwd(k, d):
        return remote(
            ubuf.at[row(2 - d, d), ucol(k)], ubuf.at[far_rows(d), ucol(k)], u_fwd_s.at[k, d], u_fwd_r.at[k, d], ynb[d]
        )

    def own_mine(k):
        for d in range(2):
            u_own(k, d, True).start()

    def own_theirs(k):
        u_sib(k).wait_recv()
        for d in range(2):
            u_own(k, d, False).start()

    def pass_on(k):
        for d in range(2):
            u_fwd(k, d).start()

    def w_load(p):
        place = aligned(p * cw, cw)
        return [
            pltpu.make_async_copy(weight_in.at[:, place], weight.at[:, place], w_loc.at[p, 0]),
            pltpu.make_async_copy(noise_in.at[:, place], noise.at[:, place], w_loc.at[p, 1]),
        ]

    def wref(hi, first, count, side, p):
        return wbuf.at[aligned(hi * blk + first, count), aligned(side * quarter + p * cw, cw)]

    def w_own(p, d):
        return remote(
            wref(zh, d * half, half, 0, p), wref(zh, d * half, half, 1, p), w_own_s.at[p, d], w_own_r.at[p, d], znb[d]
        )

    def w_leaf(p, d):
        first = (1 - d) * half
        return remote(
            wref(zh, first, half, 0, p), wref(zh, first, half, 1, p), w_leaf_s.at[p, d], w_leaf_r.at[p, d], znb[d]
        )

    def held(plane, d, u):
        i = ((plane - 1) * 2 + d) * 2 + u
        return wbuf.at[aligned((i // 8) * half, half), aligned((i % 8) * cw, cw)]

    def w_off(d, u):
        to = at(0, y, z + 1 + 2 * d, c)
        return remote(
            wref(zh, (1 - d) * half, half, 0, u + 2), held(x, d, u), w_leaf_s.at[u + 2, d], w_off_r.at[x - 1, d, u], to
        )

    def w_back(plane, d, u):
        dst = wref(zside[1 - d], (1 - d) * half, half, 1, u + 2)
        return remote(
            held(plane, d, u), dst, w_off_s.at[plane - 1, d, u], w_leaf_r.at[u + 2, d], at(plane, y, z, c)
        )

    def w_off_wait(plane, d, u):
        ref = held(plane, d, u)
        return remote(ref, ref, w_off_s.at[plane - 1, d, u], w_off_r.at[plane - 1, d, u], sib)

    def w_fwd(p, d):
        hi = zside[1 - d]
        return remote(
            wref(hi, d * half, half, 1, p), wref(hi, d * half, half, 0, p), w_fwd_s.at[p, d], w_fwd_r.at[p, d], znb[d]
        )

    def w_pass_on(p):
        for d in range(2):
            w_own(p, d).wait_recv()
            w_fwd(p, d).start()

    def clip_weights(p):
        for one in w_load(p):
            one.wait()

        @pl.when(x > 0)
        def _():
            clip_columns(p)

    def clip_columns(p):
        def body(i):
            for j in range(tiles):
                bound = levels[i, p * tiles + j].astype(jnp.float32) * clip_step
                place = (aligned(i * TILE, TILE), aligned(p * cw + j * TILE, TILE))
                noisy = weight[place].astype(jnp.float32) + noise[place].astype(jnp.float32)
                wbuf[aligned(zh * blk + i * TILE, TILE), aligned(p * cw + j * TILE, TILE)] = jnp.minimum(
                    jnp.maximum(noisy, -bound), bound
                ).astype(jnp.bfloat16)

        each(blk // TILE, body)

    def c_load(t):
        slot, other = t // 2, t % 2
        rel = (0, 1, 3, 2)[slot]
        place = (pl.ds(slot * tok, tok), pl.ds(other * blk, blk))
        src = ((y + rel) % 4, (zh + other) % 2)
        return [
            pltpu.make_async_copy(saved.at[(0, *src)], bsend.at[place], c_loc.at[t, 0]),
            pltpu.make_async_copy(saved.at[(1, *src)], bout.at[place], c_loc.at[t, 1]),
        ]

    def ccol(hi):
        return aligned(hi * blk, blk)

    def c_opp(part):
        src = (pl.ds(0, near), pl.ds(near, far))[part]
        dst = (near_rows(c), far_rows(c))[part]
        return remote(
            bout.at[src, pl.ds(blk, blk)], cbuf.at[dst, ccol(zh)], c_opp_s.at[part], c_opp_r.at[part], opp
        )

    def c_sib(part):
        ref = cbuf.at[(near_rows(c), far_rows(c))[part]]
        return remote(ref, ref, c_sib_s.at[part], c_sib_r.at[part], sib)

    def pick_batch():
        for t in range(8):
            for one in c_load(t):
                one.wait()
        second = plan[x].astype(jnp.float32)
        first = 1.0 - second

        def picked(place):
            return (
                bsend[place].astype(jnp.float32) * first + bout[place].astype(jnp.float32) * second
            ).astype(jnp.bfloat16)

        for slot in range(4):
            begin = c * near + slot * tok if slot < 3 else 2 * near + c * far

            def body(i):
                src = aligned(slot * tok + i * 16, 16, 16)
                cbuf[aligned(begin + i * 16, 16, 16), ccol(zh)] = picked((src, pl.ds(0, blk)))
                other = (src, pl.ds(blk, blk))
                bout[other] = picked(other)

            each(tok // 16, body)

    def turn(t):
        place = aligned(t * TILE, TILE)
        ctbuf[:, place] = cbuf[place, :].T

    def grad_chunk(k):
        for d in range(2):
            u_fwd(k, d).wait_recv()

        def body(t):
            b, n = t // 2, t % 2
            hi = (b + zh + (k % 2) * zl) % 2
            cols = aligned((k % 2) * quarter + (k // 2) * cw + n * 256, 256)
            gbuf[k, b, :, aligned(n * 256, 256)] = jnp.dot(
                ctbuf[aligned(hi * blk, blk), :], ubuf[:, cols], preferred_element_type=jnp.float32
            ).astype(jnp.bfloat16)

        each(4, body)

        @pl.when(k % 2 == 0)
        def _():
            for d in range(2):
                g_half(k // 2, d).start()

    def g_half(s, d):
        return remote(
            gbuf.at[2 * s, 1, pl.ds(d * half, half)], ghalf.at[d, s], g_half_s.at[s, d], g_half_r.at[s, d], znb[d]
        )

    def g_full(s, d):
        return remote(gbuf.at[2 * s + 1, d], gfull.at[d, s], g_full_s.at[s, d], g_full_r.at[s, d], znb[d])

    def combine(s):
        for d in range(2):
            g_half(s, d).wait_recv()
            for i in range(half // 64):
                inner = pl.ds(i * 64, 64)
                place = pl.ds(d * half + i * 64, 64)
                gbuf[2 * s + 1, d, place] = (
                    gbuf[2 * s + 1, d, place].astype(jnp.float32) + ghalf[d, s, inner].astype(jnp.float32)
                ).astype(jnp.bfloat16)
            g_full(s, d).start()

    def master_copy(s):
        return pltpu.make_async_copy(ready.at[s], master.at[:, aligned(s * cw, cw)], m_out.at[s])

    def finish(s):
        for d in range(2):
            g_full(s, d).wait_recv()
        scale = 1.0 / (float(rows) * 8.0) ** 0.5

        def body(i):
            line = aligned(i * TILE, TILE)
            for j in range(tiles):
                bound = levels[i, s * tiles + j].astype(jnp.float32) * clip_step
                place = (line, aligned(s * cw + j * TILE, TILE))
                noisy = weight[place].astype(jnp.float32) + noise[place].astype(jnp.float32)
                inner = pl.ds(j * TILE, TILE)
                total = gbuf[2 * s, 0, line, inner].astype(jnp.float32) + gfull[0, s, line, inner].astype(jnp.float32)
                total = total + gfull[1, s, line, inner].astype(jnp.float32)
                ready[s, line, inner] = jnp.where(jnp.abs(noisy) <= bound, total * scale, 0.0)

        each(blk // TILE, body)
        master_copy(s).start()

    def w_ready(p):
        for d in range(2):
            w_leaf(p, d).wait_recv()
            w_fwd(p, d).wait_recv()

    def tile_branch(place, n, sides):
        total = None
        for cols in sides:
            term = lax.dot_general(
                ubuf[place, cols],
                wbuf[aligned(n * 256, 256), cols],
                (((1,), (1,)), ((), ())),
                preferred_element_type=jnp.float32,
            )
            total = term if total is None else total + term
        return total

    def sides_of(s):
        return [aligned(side * quarter + s * cw, cw) for side in range(2)]

    def branch_near(s):
        w_ready(s)

        def body(t):
            place, cols = near_rows(t // 4), aligned((t % 4) * 256, 256)
            acc[place, cols] += tile_branch(place, t % 4, sides_of(s))

        each(2 * (feats // 256), body)

    parts = ((0, tok, (0,)), (tok, 2 * tok, (1, 2)), (near, far, (3,)))

    def b_sib(part, n):
        first, count, _ = parts[part]
        place = (pl.ds(first, count), aligned(n * 256, 256))
        return remote(bsend.at[place], brecv.at[place], b_sib_s.at[part, n], b_sib_r.at[part, n], sib)

    def b_out(n, slot):
        yt = (y + (0, 1, 3, 2)[slot]) % 4
        return remote(
            bout.at[pl.ds(slot * tok, tok), aligned(n * 256, 256)],
            passed.at[:, aligned(y * feats + n * 256, 256)],
            b_out_s.at[n, slot], b_out_r.at[n, slot], at(x + 3, yt, z, c),
        )

    def branch_send(part):
        first, count, slots = parts[part]

        def value(cc, n):
            cols = aligned(n * 256, 256)
            if part == 2:
                return acc[aligned(cc * far, far, 16), cols]
            place = aligned(cc * near + first, count, 16)
            return acc[place, cols] + tile_branch(place, n, sides_of(subs - 1))

        def theirs(n):
            bsend[pl.ds(first, count), aligned(n * 256, 256)] = value(oc, n).astype(jnp.bfloat16)
            b_sib(part, n).start()

        def send(n):
            for slot in slots:
                b_out(n, slot).start()

        def ours(n):
            cols = aligned(n * 256, 256)
            total = value(c, n)
            b_sib(part, n).wait_recv()
            total = total + brecv[pl.ds(first, count), cols].astype(jnp.float32)
            bout[pl.ds(first, count), cols] = total.astype(jnp.bfloat16)
            send(n)

        @pl.when(x > 0)
        def _():
            each(feats // 256, theirs)
            each(feats // 256, ours)

        @pl.when(x == 0)
        def _():
            bout[pl.ds(first, count), :] = jnp.zeros((count, feats), jnp.bfloat16)
            each(feats // 256, send)

    def branch_far():
        whole = pl.ds(2 * near, 2 * far)

        def body(n):
            acc[pl.ds(0, 2 * far), aligned(n * 256, 256)] = tile_branch(
                whole, n, [pl.ds(i * quarter, quarter) for i in range(2)]
            )

        each(feats // 256, body)

    for t in range(8):
        for one in c_load(t):
            one.start()
    clip_weights(0)
    for p in range(1, subs):
        for one in w_load(p):
            one.start()
    pl.semaphore_wait(barrier, greeted)
    for k in range(2):
        own_mine(k)
        u_sib(k).start()

    @pl.when(x > 0)
    def _():
        for d in range(2):
            w_own(0, d).start()
            w_leaf(0, d).start()

    pick_batch()
    for part in range(2):
        c_opp(part).start()
    for k in range(2):
        own_theirs(k)
    for p in (2, 3):
        clip_weights(p)

    @pl.when(x > 0)
    def _():
        for d in range(2):
            w_off(d, 0).start()

    each(chunks - 2, lambda k: u_sib(k + 2).start())
    each(chunks, lambda k: u_local(k).start())
    clip_weights(1)
    acc[...] = jnp.zeros_like(acc)

    def step(k):
        @pl.when(k < chunks)
        def _():
            for d in range(2):
                u_own_wait(k, d, d).wait_recv()

            @pl.when(k >= ahead - 1)
            def _():
                pass_on(k - (ahead - 1))

            @pl.when(k + 2 < chunks)
            def _():
                own_mine(k + 2)
                own_theirs(k + 2)

            @pl.when(k == chunks - 1)
            def _():
                each(ahead - 1, lambda i: pass_on(chunks - ahead + 1 + i))

            u_local(k).wait()
            for d in range(2):
                u_own_wait(k, d, 1 - d).wait_recv()

        @pl.when((x == 0) & ((k == 2) | (k == 4)))
        def _():
            u = (k - 2) // 2
            for plane in (1, 3, 2):
                for d in range(2):
                    w_off_wait(plane, d, u).wait_recv()
                    w_back(plane, d, u).start()

        @pl.when((x > 0) & (k == 0))
        def _():
            for d in range(2):
                w_off(d, 1).start()

        @pl.when((x > 0) & (k == 1))
        def _():
            w_pass_on(0)

        @pl.when((x > 0) & (k == 2))
        def _():
            for d in range(2):
                w_own(1, d).start()
                w_leaf(1, d).start()
                w_own(2, d).start()

        @pl.when((x > 0) & (k == 3))
        def _():
            for d in range(2):
                w_own(3, d).start()

        @pl.when(k == 3)
        def _():
            for part in range(2):
                c_opp(part).wait_recv()
                c_sib(part).start()
            for part in range(2):
                c_sib(part).wait_recv()
            each((2 * rows) // TILE, turn)

        @pl.when((x > 0) & (k == 4))
        def _():
            w_pass_on(1)
            w_pass_on(2)

        @pl.when((x > 0) & (k == 5))
        def _():
            w_pass_on(3)

        @pl.when(k == 7)
        def _():
            for part in range(2):
                c_opp(part).wait_send()

            @pl.when(x > 0)
            def _():
                w_ready(subs - 1)

            branch_send(0)

        @pl.when((k >= 3) & (k != 7))
        def _():
            grad_chunk(k - 3)

        @pl.when((x > 0) & (k >= 4) & (k < 7))
        def _():
            branch_near(k - 4)

        @pl.when((k == 5) | (k == 7) | (k == 9))
        def _():
            combine((k - 5) // 2)

        @pl.when(k == 7)
        def _():
            branch_send(1)
            grad_chunk(4)

    each(chunks + 3, step)

    @pl.when(x > 0)
    def _():
        branch_far()

    branch_send(2)
    combine(3)

    for part in range(2):
        c_sib(part).wait_send()

    def drain_u(k):
        u_sib(k).wait_send()
        for d in range(2):
            for cc in range(2):
                u_own_wait(k, d, cc).wait_send()
            u_fwd(k, d).wait_send()

    each(chunks, drain_u)

    def drain(s):
        for d in range(2):
            g_half(s, d).wait_send()

        @pl.when(x > 0)
        def _():
            for d in range(2):
                w_own(s, d).wait_send()
                w_leaf(s, d).wait_send()
                w_fwd(s, d).wait_send()
            for part in range(3):
                b_sib(part, s).wait_send()

    each(subs, drain)

    @pl.when(x == 0)
    def _():
        for plane in range(1, 4):
            for d in range(2):
                for u in range(2):
                    w_back(plane, d, u).wait_send()

    each(subs - 1, finish)

    def drain_last(s):
        for slot in range(4):
            b_out(s, slot).wait()

    each(subs, drain_last)
    for s in range(subs - 1):
        master_copy(s).wait()
    finish(subs - 1)
    for s in range(subs):
        for d in range(2):
            g_full(s, d).wait_send()
    master_copy(subs - 1).wait()


def relay_call(up, saved, weight, noise, levels, plan):
    tok, width = up.shape
    blk, quarter = weight.shape
    rows = 4 * tok
    brick, feats = 2 * rows, 2 * blk
    span = 2 * quarter
    cw = quarter // 4
    bf, f32 = jnp.bfloat16, jnp.float32
    dma = pltpu.SemaphoreType.DMA
    sems = [
        (8,), (8,), (8,), (8, 2, 2), (8, 2, 2), (8, 2), (8, 2),
        (8, 2), (2,), (2,), (2,), (2,),
        (4, 2), (4, 2), (4, 2), (4, 2), (4, 2), (4, 2), (4, 2), (3, 2, 2), (3, 2, 2),
        (4, 2), (4, 2), (4, 2), (4, 2),
        (3, 4), (3, 4), (4, 4), (4, 4), (4,),
    ]
    flops = 2 * 2 * brick * feats * span
    anywhere = pl.BlockSpec(memory_space=pl.ANY)
    scalars = pl.BlockSpec(memory_space=pltpu.SMEM)
    return pl.pallas_call(
        relay_kernel,
        out_shape=(jax.ShapeDtypeStruct((blk, quarter), f32), jax.ShapeDtypeStruct((tok, 4 * feats), bf)),
        in_specs=[anywhere, anywhere, anywhere, anywhere, scalars, scalars],
        out_specs=(anywhere, anywhere),
        scratch_shapes=[
            pltpu.VMEM((brick, span), bf),
            pltpu.VMEM((feats, span), bf),
            pltpu.VMEM((brick, feats), bf),
            pltpu.VMEM((feats, brick), bf),
            pltpu.VMEM((6 * tok, feats), f32),
            pltpu.VMEM((8, 2, blk, cw), bf),
            pltpu.VMEM((2, 4, blk // 2, cw), bf),
            pltpu.VMEM((2, 4, blk, cw), bf),
            pltpu.VMEM((4, blk, cw), f32),
            pltpu.VMEM((rows, feats), bf),
            pltpu.VMEM((rows, feats), bf),
            pltpu.VMEM((rows, feats), bf),
            pltpu.VMEM((blk, quarter), bf),
            pltpu.VMEM((blk, quarter), bf),
        ]
        + [dma(shape) for shape in sems],
        compiler_params=pltpu.CompilerParams(
            collective_id=0, has_side_effects=True, vmem_limit_bytes=63 * 1024 * 1024
        ),
        cost_estimate=pl.CostEstimate(flops=flops, bytes_accessed=32 * 1024 * 1024, transcendentals=0),
        name="relay",
    )(up, saved, weight, noise, levels, plan)


def hand_over(grad, arrived):
    pieces = []
    for which, one in enumerate((grad, arrived)):
        size = -(-one.shape[0] // (32, 32)[which]) * 16
        pieces += [
            (which, pl.ds(begin, min(size, one.shape[0] - begin))) for begin in range(0, one.shape[0], size)
        ]

    def kernel(grad_in, arrived_in, grad_out, arrived_out, grad_held, arrived_held, load_sem, store_sem):
        routes = ((grad_in, grad_held, grad_out), (arrived_in, arrived_held, arrived_out))
        loads, stores = [], []
        for i, (which, place) in enumerate(pieces):
            src, held, dst = (ref.at[place] for ref in routes[which])
            loads.append(pltpu.make_async_copy(src, held, load_sem.at[i]))
            stores.append(pltpu.make_async_copy(held, dst, store_sem.at[i]))
        for one in loads:
            one.start()
        for load, store in zip(loads, stores):
            load.wait()
            store.start()
        for one in stores:
            one.wait()

    anywhere = pl.BlockSpec(memory_space=pl.ANY)
    return pl.pallas_call(
        kernel,
        out_shape=tuple(jax.ShapeDtypeStruct(one.shape, one.dtype) for one in (grad, arrived)),
        in_specs=[anywhere, anywhere],
        out_specs=(anywhere, anywhere),
        scratch_shapes=[pltpu.VMEM(one.shape, one.dtype) for one in (grad, arrived)]
        + [pltpu.SemaphoreType.DMA((len(pieces),)), pltpu.SemaphoreType.DMA((len(pieces),))],
        compiler_params=pltpu.CompilerParams(vmem_limit_bytes=63 * 1024 * 1024),
        name="hand_over",
    )(grad, arrived)


def local(upstream, saved_input, weight, weight_noise, levels, plan):
    tok = upstream.shape[1]
    blk = weight.shape[1]
    saved = saved_input.reshape(saved_input.shape[1], 4, 2, tok, blk)
    grad, arrived = relay_call(upstream[0], saved, weight[0], weight_noise[0], levels[0], plan)
    master, passed = hand_over(grad, arrived)
    return (master[None], passed[None])


def solution(mesh):
    placed = (
        P("pipe", ("dp", "tp"), None),
        P("pipe", None, "dp", "tp"),
        P("pipe", "tp", "dp"),
        P("pipe", "tp", "dp"),
        P("pipe", "tp", "dp"),
        P(),
    )
    return jax.shard_map(
        local,
        mesh=mesh,
        in_specs=placed,
        out_specs=(P("pipe", "tp", "dp"), P("pipe", ("dp", "tp"), None)),
        check_vma=False,
    )
```

```python
import jax
import jax.numpy as jnp
from jax import lax
from jax.experimental import pallas as pl
from jax.experimental.pallas import tpu as pltpu
from jax.sharding import PartitionSpec as P

clip_step = 0.006
MESH = pl.DeviceIdType.MESH
TILE = 128


def aligned(start, size, step=128):
    return pl.ds(pl.multiple_of(start, step), size)


def relay_kernel(
    up, saved, weight_in, noise_in, levels, plan,
    master, passed,
    ubuf, wbuf, cbuf, ctbuf, acc, gbuf, ghalf, gfull, ready, bsend, brecv, bout, weight, noise,
    u_loc, u_sib_s, u_sib_r, u_own_s, u_own_r, u_fwd_s, u_fwd_r,
    c_loc, c_opp_s, c_opp_r, c_sib_s, c_sib_r,
    w_loc, w_own_s, w_own_r, w_leaf_s, w_leaf_r, w_fwd_s, w_fwd_r, w_off_s, w_off_r,
    g_half_s, g_half_r, g_full_s, g_full_r,
    b_sib_s, b_sib_r, b_out_s, b_out_r, m_out,
):
    tok = up.shape[0]
    rows = tok * 4
    near, far = 3 * tok, tok
    quarter = weight.shape[1]
    blk = weight.shape[0]
    half = blk // 2
    subs = 4
    chunks = 2 * subs
    cw = quarter // subs
    tiles = cw // TILE
    feats = 2 * blk
    ahead = 3

    x = lax.axis_index("pipe")
    tp = lax.axis_index("tp")
    dp = lax.axis_index("dp")
    y, zh = tp // 2, tp % 2
    zl, c = dp // 2, dp % 2
    z = 2 * zh + zl
    oc = 1 - c

    def at(xx, yy, zz, cc):
        xx, yy, zz = xx % 4, yy % 4, zz % 4
        return (xx, yy * 2 + zz // 2, (zz % 2) * 2 + cc)

    sib = at(x, y, z, oc)
    opp = at(x, y, z + 2, c)
    ynb = (at(x, y + 1, z, c), at(x, y + 3, z, c))
    znb = (at(x, y, z + 1, c), at(x, y, z + 3, c))
    zp = (zh + zl) % 2
    zside = (zp, 1 - zp)

    for place in (pl.ds(0, cw),):
        pltpu.make_async_copy(weight_in.at[:, place], weight.at[:, place], w_loc.at[0, 0]).start()
        pltpu.make_async_copy(noise_in.at[:, place], noise.at[:, place], w_loc.at[0, 1]).start()

    barrier = pltpu.get_barrier_semaphore()
    greet = [sib, opp, *ynb, *znb] + [at(x + 1, y + j, z, c) for j in range(4)]
    for one in greet:
        pl.semaphore_signal(barrier, inc=1, device_id=one, device_id_type=MESH)

    @pl.when(x > 0)
    def _():
        pl.semaphore_signal(barrier, inc=1, device_id=at(0, y, z, c), device_id_type=MESH)

    @pl.when(x == 0)
    def _():
        for plane in range(1, 4):
            for step in (1, 3):
                pl.semaphore_signal(barrier, inc=1, device_id=at(plane, y, z + step, c), device_id_type=MESH)

    greeted = len(greet) + 3 - (x + 3) // 4

    def remote(src, dst, s, r, to):
        return pltpu.make_async_remote_copy(
            src_ref=src, dst_ref=dst, send_sem=s, recv_sem=r, device_id=to, device_id_type=MESH
        )

    def each(count, body):
        def one(i, _):
            body(i)
            return 0

        lax.fori_loop(0, count, one, 0)

    def near_rows(cc):
        return aligned(cc * near, near, 16)

    def far_rows(cc):
        return aligned(2 * near + cc * far, far, 16)

    def row(slot, cc):
        return aligned(cc * near + slot * tok, tok, 16)

    def ucol(k):
        return aligned((k % 2) * quarter + (k // 2) * cw, cw)

    def hcol(k, cc):
        return aligned(((zl + k) % 2) * (2 * quarter) + cc * quarter + (k // 2) * cw, cw)

    def u_local(k):
        return pltpu.make_async_copy(up.at[:, hcol(k, c)], ubuf.at[row(0, c), ucol(k)], u_loc.at[k])

    def u_sib(k):
        return remote(up.at[:, hcol(k, oc)], ubuf.at[row(0, c), ucol(k)], u_sib_s.at[k], u_sib_r.at[k], sib)

    def u_own(k, d, mine):
        cc = c if mine else oc
        src = up.at[:, hcol(k, c)] if mine else ubuf.at[row(0, oc), ucol(k)]
        return remote(src, ubuf.at[row(2 - d, cc), ucol(k)], u_own_s.at[k, d, cc], u_own_r.at[k, d, cc], ynb[d])

    def u_own_wait(k, d, cc):
        ref = ubuf.at[row(2 - d, cc), ucol(k)]
        return remote(ref, ref, u_own_s.at[k, d, cc], u_own_r.at[k, d, cc], ynb[d])

    def u_fwd(k, d):
        return remote(
            ubuf.at[row(2 - d, d), ucol(k)], ubuf.at[far_rows(d), ucol(k)], u_fwd_s.at[k, d], u_fwd_r.at[k, d], ynb[d]
        )

    def own_mine(k):
        for d in range(2):
            u_own(k, d, True).start()

    def own_theirs(k):
        u_sib(k).wait_recv()
        for d in range(2):
            u_own(k, d, False).start()

    def pass_on(k):
        for d in range(2):
            u_fwd(k, d).start()

    def w_load(p):
        place = aligned(p * cw, cw)
        return [
            pltpu.make_async_copy(weight_in.at[:, place], weight.at[:, place], w_loc.at[p, 0]),
            pltpu.make_async_copy(noise_in.at[:, place], noise.at[:, place], w_loc.at[p, 1]),
        ]

    def wref(hi, first, count, side, p):
        return wbuf.at[aligned(hi * blk + first, count), aligned(side * quarter + p * cw, cw)]

    def w_own(p, d):
        return remote(
            wref(zh, d * half, half, 0, p), wref(zh, d * half, half, 1, p), w_own_s.at[p, d], w_own_r.at[p, d], znb[d]
        )

    def w_leaf(p, d):
        first = (1 - d) * half
        return remote(
            wref(zh, first, half, 0, p), wref(zh, first, half, 1, p), w_leaf_s.at[p, d], w_leaf_r.at[p, d], znb[d]
        )

    def held(plane, d, u):
        i = ((plane - 1) * 2 + d) * 2 + u
        return wbuf.at[aligned((i // 8) * half, half), aligned((i % 8) * cw, cw)]

    def w_off(d, u):
        to = at(0, y, z + 1 + 2 * d, c)
        return remote(
            wref(zh, (1 - d) * half, half, 0, u + 2), held(x, d, u), w_leaf_s.at[u + 2, d], w_off_r.at[x - 1, d, u], to
        )

    def w_back(plane, d, u):
        dst = wref(zside[1 - d], (1 - d) * half, half, 1, u + 2)
        return remote(
            held(plane, d, u), dst, w_off_s.at[plane - 1, d, u], w_leaf_r.at[u + 2, d], at(plane, y, z, c)
        )

    def w_off_wait(plane, d, u):
        ref = held(plane, d, u)
        return remote(ref, ref, w_off_s.at[plane - 1, d, u], w_off_r.at[plane - 1, d, u], sib)

    def w_fwd(p, d):
        hi = zside[1 - d]
        return remote(
            wref(hi, d * half, half, 1, p), wref(hi, d * half, half, 0, p), w_fwd_s.at[p, d], w_fwd_r.at[p, d], znb[d]
        )

    def w_pass_on(p):
        for d in range(2):
            w_own(p, d).wait_recv()
            w_fwd(p, d).start()

    def clip_weights(p):
        for one in w_load(p):
            one.wait()

        @pl.when(x > 0)
        def _():
            clip_columns(p)

    def clip_columns(p):
        def body(i):
            for j in range(tiles):
                bound = levels[i, p * tiles + j].astype(jnp.float32) * clip_step
                place = (aligned(i * TILE, TILE), aligned(p * cw + j * TILE, TILE))
                noisy = weight[place].astype(jnp.float32) + noise[place].astype(jnp.float32)
                wbuf[aligned(zh * blk + i * TILE, TILE), aligned(p * cw + j * TILE, TILE)] = jnp.minimum(
                    jnp.maximum(noisy, -bound), bound
                ).astype(jnp.bfloat16)

        each(blk // TILE, body)

    def c_load(t):
        slot, other = t // 2, t % 2
        rel = (0, 1, 3, 2)[slot]
        place = (pl.ds(slot * tok, tok), pl.ds(other * blk, blk))
        src = ((y + rel) % 4, (zh + other) % 2)
        return [
            pltpu.make_async_copy(saved.at[(0, *src)], bsend.at[place], c_loc.at[t, 0]),
            pltpu.make_async_copy(saved.at[(1, *src)], bout.at[place], c_loc.at[t, 1]),
        ]

    def ccol(hi):
        return aligned(hi * blk, blk)

    def c_opp(part):
        src = (pl.ds(0, near), pl.ds(near, far))[part]
        dst = (near_rows(c), far_rows(c))[part]
        return remote(
            bout.at[src, pl.ds(blk, blk)], cbuf.at[dst, ccol(zh)], c_opp_s.at[part], c_opp_r.at[part], opp
        )

    def c_sib(part):
        ref = cbuf.at[(near_rows(c), far_rows(c))[part]]
        return remote(ref, ref, c_sib_s.at[part], c_sib_r.at[part], sib)

    def pick_batch():
        for t in range(8):
            for one in c_load(t):
                one.wait()
        second = plan[x].astype(jnp.float32)
        first = 1.0 - second

        def picked(place):
            return (
                bsend[place].astype(jnp.float32) * first + bout[place].astype(jnp.float32) * second
            ).astype(jnp.bfloat16)

        for slot in range(4):
            begin = c * near + slot * tok if slot < 3 else 2 * near + c * far

            def body(i):
                src = aligned(slot * tok + i * 16, 16, 16)
                cbuf[aligned(begin + i * 16, 16, 16), ccol(zh)] = picked((src, pl.ds(0, blk)))
                other = (src, pl.ds(blk, blk))
                bout[other] = picked(other)

            each(tok // 16, body)

    def turn(t):
        place = aligned(t * TILE, TILE)
        ctbuf[:, place] = cbuf[place, :].T

    def grad_chunk(k):
        for d in range(2):
            u_fwd(k, d).wait_recv()

        def body(t):
            b, n = t // 2, t % 2
            hi = (b + zh + (k % 2) * zl) % 2
            cols = aligned((k % 2) * quarter + (k // 2) * cw + n * 256, 256)
            gbuf[k, b, :, aligned(n * 256, 256)] = jnp.dot(
                ctbuf[aligned(hi * blk, blk), :], ubuf[:, cols], preferred_element_type=jnp.float32
            ).astype(jnp.bfloat16)

        each(4, body)

        @pl.when(k % 2 == 0)
        def _():
            for d in range(2):
                g_half(k // 2, d).start()

    def g_half(s, d):
        return remote(
            gbuf.at[2 * s, 1, pl.ds(d * half, half)], ghalf.at[d, s], g_half_s.at[s, d], g_half_r.at[s, d], znb[d]
        )

    def g_full(s, d):
        return remote(gbuf.at[2 * s + 1, d], gfull.at[d, s], g_full_s.at[s, d], g_full_r.at[s, d], znb[d])

    def combine(s):
        for d in range(2):
            g_half(s, d).wait_recv()
            for i in range(half // 64):
                inner = pl.ds(i * 64, 64)
                place = pl.ds(d * half + i * 64, 64)
                gbuf[2 * s + 1, d, place] = (
                    gbuf[2 * s + 1, d, place].astype(jnp.float32) + ghalf[d, s, inner].astype(jnp.float32)
                ).astype(jnp.bfloat16)
            g_full(s, d).start()

    def master_copy(s, i):
        line = aligned(i * TILE, TILE)
        return pltpu.make_async_copy(ready.at[s, line], master.at[line, aligned(s * cw, cw)], m_out.at[s, i])

    def finish(s):
        for d in range(2):
            g_full(s, d).wait_recv()
        scale = 1.0 / (float(rows) * 8.0) ** 0.5

        def body(i):
            line = aligned(i * TILE, TILE)
            for j in range(tiles):
                bound = levels[i, s * tiles + j].astype(jnp.float32) * clip_step
                place = (line, aligned(s * cw + j * TILE, TILE))
                noisy = weight[place].astype(jnp.float32) + noise[place].astype(jnp.float32)
                inner = pl.ds(j * TILE, TILE)
                total = gbuf[2 * s, 0, line, inner].astype(jnp.float32) + gfull[0, s, line, inner].astype(jnp.float32)
                total = total + gfull[1, s, line, inner].astype(jnp.float32)
                ready[s, line, inner] = jnp.where(jnp.abs(noisy) <= bound, total * scale, 0.0)
            master_copy(s, i).start()

        each(blk // TILE, body)

    def w_ready(p):
        for d in range(2):
            w_leaf(p, d).wait_recv()
            w_fwd(p, d).wait_recv()

    def tile_branch(place, n, sides):
        total = None
        for cols in sides:
            term = lax.dot_general(
                ubuf[place, cols],
                wbuf[aligned(n * 256, 256), cols],
                (((1,), (1,)), ((), ())),
                preferred_element_type=jnp.float32,
            )
            total = term if total is None else total + term
        return total

    def sides_of(s):
        return [aligned(side * quarter + s * cw, cw) for side in range(2)]

    def branch_near(s):
        w_ready(s)

        def body(t):
            place, cols = near_rows(t // 4), aligned((t % 4) * 256, 256)
            acc[place, cols] += tile_branch(place, t % 4, sides_of(s))

        each(2 * (feats // 256), body)

    parts = ((0, tok, (0,)), (tok, 2 * tok, (1, 2)), (near, far, (3,)))

    def b_sib(part, n):
        first, count, _ = parts[part]
        place = (pl.ds(first, count), aligned(n * 256, 256))
        return remote(bsend.at[place], brecv.at[place], b_sib_s.at[part, n], b_sib_r.at[part, n], sib)

    def b_out(n, slot):
        yt = (y + (0, 1, 3, 2)[slot]) % 4
        return remote(
            bout.at[pl.ds(slot * tok, tok), aligned(n * 256, 256)],
            passed.at[:, aligned(y * feats + n * 256, 256)],
            b_out_s.at[n, slot], b_out_r.at[n, slot], at(x + 3, yt, z, c),
        )

    def branch_send(part):
        first, count, slots = parts[part]

        def value(cc, n):
            cols = aligned(n * 256, 256)
            if part == 2:
                return acc[aligned(cc * far, far, 16), cols]
            place = aligned(cc * near + first, count, 16)
            return acc[place, cols] + tile_branch(place, n, sides_of(subs - 1))

        def theirs(n):
            bsend[pl.ds(first, count), aligned(n * 256, 256)] = value(oc, n).astype(jnp.bfloat16)
            b_sib(part, n).start()

        def send(n):
            for slot in slots:
                b_out(n, slot).start()

        def ours(n):
            cols = aligned(n * 256, 256)
            total = value(c, n)
            b_sib(part, n).wait_recv()
            total = total + brecv[pl.ds(first, count), cols].astype(jnp.float32)
            bout[pl.ds(first, count), cols] = total.astype(jnp.bfloat16)
            send(n)

        @pl.when(x > 0)
        def _():
            each(feats // 256, theirs)
            each(feats // 256, ours)

        @pl.when(x == 0)
        def _():
            bout[pl.ds(first, count), :] = jnp.zeros((count, feats), jnp.bfloat16)
            each(feats // 256, send)

    def branch_far():
        whole = pl.ds(2 * near, 2 * far)

        def body(n):
            acc[pl.ds(0, 2 * far), aligned(n * 256, 256)] = tile_branch(
                whole, n, [pl.ds(i * quarter, quarter) for i in range(2)]
            )

        each(feats // 256, body)

    for t in range(8):
        for one in c_load(t):
            one.start()
    clip_weights(0)
    for p in range(1, subs):
        for one in w_load(p):
            one.start()
    pl.semaphore_wait(barrier, greeted)
    for k in range(2):
        own_mine(k)
        u_sib(k).start()

    @pl.when(x > 0)
    def _():
        for d in range(2):
            w_own(0, d).start()
            w_leaf(0, d).start()

    pick_batch()
    for part in range(2):
        c_opp(part).start()
    for k in range(2):
        own_theirs(k)
    for p in (2, 3):
        clip_weights(p)

    @pl.when(x > 0)
    def _():
        for u in range(2):
            for d in range(2):
                w_off(d, u).start()

    each(chunks - 2, lambda k: u_sib(k + 2).start())
    each(chunks, lambda k: u_local(k).start())
    clip_weights(1)
    acc[...] = jnp.zeros_like(acc)

    def step(k):
        @pl.when(k < chunks)
        def _():
            for d in range(2):
                u_own_wait(k, d, d).wait_recv()

            @pl.when(k >= ahead - 1)
            def _():
                pass_on(k - (ahead - 1))

            @pl.when(k + 2 < chunks)
            def _():
                own_mine(k + 2)
                own_theirs(k + 2)

            @pl.when(k == chunks - 1)
            def _():
                each(ahead - 1, lambda i: pass_on(chunks - ahead + 1 + i))

            u_local(k).wait()
            for d in range(2):
                u_own_wait(k, d, 1 - d).wait_recv()

        @pl.when((x == 0) & ((k == 2) | (k == 4)))
        def _():
            u = (k - 2) // 2
            for plane in (1, 3, 2):
                for d in range(2):
                    w_off_wait(plane, d, u).wait_recv()
                    w_back(plane, d, u).start()

        @pl.when((x > 0) & (k == 1))
        def _():
            w_pass_on(0)

        @pl.when((x > 0) & (k == 2))
        def _():
            for d in range(2):
                w_own(1, d).start()
                w_leaf(1, d).start()
                w_own(2, d).start()

        @pl.when((x > 0) & (k == 3))
        def _():
            for d in range(2):
                w_own(3, d).start()

        @pl.when(k == 3)
        def _():
            for part in range(2):
                c_opp(part).wait_recv()
                c_sib(part).start()
            for part in range(2):
                c_sib(part).wait_recv()
            each((2 * rows) // TILE, turn)

        @pl.when((x > 0) & (k == 4))
        def _():
            w_pass_on(1)
            w_pass_on(2)

        @pl.when((x > 0) & (k == 5))
        def _():
            w_pass_on(3)

        @pl.when(k == 7)
        def _():
            for part in range(2):
                c_opp(part).wait_send()

            @pl.when(x > 0)
            def _():
                w_ready(subs - 1)

            branch_send(0)

        @pl.when((k >= 3) & (k != 7))
        def _():
            grad_chunk(k - 3)

        @pl.when((x > 0) & (k >= 4) & (k < 7))
        def _():
            branch_near(k - 4)

        @pl.when((k == 5) | (k == 7) | (k == 9))
        def _():
            combine((k - 5) // 2)

        @pl.when(k == 7)
        def _():
            branch_send(1)
            grad_chunk(4)

    each(chunks + 3, step)

    @pl.when(x > 0)
    def _():
        branch_far()

    branch_send(2)
    combine(3)

    for part in range(2):
        c_sib(part).wait_send()

    def drain_u(k):
        u_sib(k).wait_send()
        for d in range(2):
            for cc in range(2):
                u_own_wait(k, d, cc).wait_send()
            u_fwd(k, d).wait_send()

    each(chunks, drain_u)

    def drain(s):
        for d in range(2):
            g_half(s, d).wait_send()

        @pl.when(x > 0)
        def _():
            for d in range(2):
                w_own(s, d).wait_send()
                w_leaf(s, d).wait_send()
                w_fwd(s, d).wait_send()
            for part in range(3):
                b_sib(part, s).wait_send()

    each(subs, drain)

    @pl.when(x == 0)
    def _():
        for plane in range(1, 4):
            for d in range(2):
                for u in range(2):
                    w_back(plane, d, u).wait_send()

    each(subs - 1, finish)

    def drain_last(s):
        for slot in range(4):
            b_out(s, slot).wait()

    each(subs, drain_last)
    for s in range(subs - 1):
        for i in range(blk // TILE):
            master_copy(s, i).wait()
    finish(subs - 1)
    for s in range(subs):
        for d in range(2):
            g_full(s, d).wait_send()
    for i in range(blk // TILE):
        master_copy(subs - 1, i).wait()


def relay_call(up, saved, weight, noise, levels, plan):
    tok, width = up.shape
    blk, quarter = weight.shape
    rows = 4 * tok
    brick, feats = 2 * rows, 2 * blk
    span = 2 * quarter
    cw = quarter // 4
    bf, f32 = jnp.bfloat16, jnp.float32
    dma = pltpu.SemaphoreType.DMA
    sems = [
        (8,), (8,), (8,), (8, 2, 2), (8, 2, 2), (8, 2), (8, 2),
        (8, 2), (2,), (2,), (2,), (2,),
        (4, 2), (4, 2), (4, 2), (4, 2), (4, 2), (4, 2), (4, 2), (3, 2, 2), (3, 2, 2),
        (4, 2), (4, 2), (4, 2), (4, 2),
        (3, 4), (3, 4), (4, 4), (4, 4), (4, 4),
    ]
    flops = 2 * 2 * brick * feats * span
    anywhere = pl.BlockSpec(memory_space=pl.ANY)
    scalars = pl.BlockSpec(memory_space=pltpu.SMEM)
    return pl.pallas_call(
        relay_kernel,
        out_shape=(jax.ShapeDtypeStruct((blk, quarter), f32), jax.ShapeDtypeStruct((tok, 4 * feats), bf)),
        in_specs=[anywhere, anywhere, anywhere, anywhere, scalars, scalars],
        out_specs=(anywhere, anywhere),
        scratch_shapes=[
            pltpu.VMEM((brick, span), bf),
            pltpu.VMEM((feats, span), bf),
            pltpu.VMEM((brick, feats), bf),
            pltpu.VMEM((feats, brick), bf),
            pltpu.VMEM((6 * tok, feats), f32),
            pltpu.VMEM((8, 2, blk, cw), bf),
            pltpu.VMEM((2, 4, blk // 2, cw), bf),
            pltpu.VMEM((2, 4, blk, cw), bf),
            pltpu.VMEM((4, blk, cw), f32),
            pltpu.VMEM((rows, feats), bf),
            pltpu.VMEM((rows, feats), bf),
            pltpu.VMEM((rows, feats), bf),
            pltpu.VMEM((blk, quarter), bf),
            pltpu.VMEM((blk, quarter), bf),
        ]
        + [dma(shape) for shape in sems],
        compiler_params=pltpu.CompilerParams(
            collective_id=0, has_side_effects=True, vmem_limit_bytes=63 * 1024 * 1024
        ),
        cost_estimate=pl.CostEstimate(flops=flops, bytes_accessed=32 * 1024 * 1024, transcendentals=0),
        name="relay",
    )(up, saved, weight, noise, levels, plan)


def hand_over(grad, arrived):
    pieces = []
    for which, one in enumerate((grad, arrived)):
        size = -(-one.shape[0] // (32, 32)[which]) * 16
        pieces += [
            (which, pl.ds(begin, min(size, one.shape[0] - begin))) for begin in range(0, one.shape[0], size)
        ]

    def kernel(grad_in, arrived_in, grad_out, arrived_out, grad_held, arrived_held, load_sem, store_sem):
        routes = ((grad_in, grad_held, grad_out), (arrived_in, arrived_held, arrived_out))
        loads, stores = [], []
        for i, (which, place) in enumerate(pieces):
            src, held, dst = (ref.at[place] for ref in routes[which])
            loads.append(pltpu.make_async_copy(src, held, load_sem.at[i]))
            stores.append(pltpu.make_async_copy(held, dst, store_sem.at[i]))
        for one in loads:
            one.start()
        for load, store in zip(loads, stores):
            load.wait()
            store.start()
        for one in stores:
            one.wait()

    anywhere = pl.BlockSpec(memory_space=pl.ANY)
    return pl.pallas_call(
        kernel,
        out_shape=tuple(jax.ShapeDtypeStruct(one.shape, one.dtype) for one in (grad, arrived)),
        in_specs=[anywhere, anywhere],
        out_specs=(anywhere, anywhere),
        scratch_shapes=[pltpu.VMEM(one.shape, one.dtype) for one in (grad, arrived)]
        + [pltpu.SemaphoreType.DMA((len(pieces),)), pltpu.SemaphoreType.DMA((len(pieces),))],
        compiler_params=pltpu.CompilerParams(vmem_limit_bytes=63 * 1024 * 1024),
        name="hand_over",
    )(grad, arrived)


def local(upstream, saved_input, weight, weight_noise, levels, plan):
    tok = upstream.shape[1]
    blk = weight.shape[1]
    saved = saved_input.reshape(saved_input.shape[1], 4, 2, tok, blk)
    grad, arrived = relay_call(upstream[0], saved, weight[0], weight_noise[0], levels[0], plan)
    master, passed = hand_over(grad, arrived)
    return (master[None], passed[None])


def solution(mesh):
    placed = (
        P("pipe", ("dp", "tp"), None),
        P("pipe", None, "dp", "tp"),
        P("pipe", "tp", "dp"),
        P("pipe", "tp", "dp"),
        P("pipe", "tp", "dp"),
        P(),
    )
    return jax.shard_map(
        local,
        mesh=mesh,
        in_specs=placed,
        out_specs=(P("pipe", "tp", "dp"), P("pipe", ("dp", "tp"), None)),
        check_vma=False,
    )
```
